256 devices in a mesh: section: 16 (over z, core), expert: 16 (over y, x).
Axes of the slice: x: 4, y: 4, z: 8, core: 2. Of those that a mesh axis runs over, the one named last changes fastest.
Arguments:
- section_layer_input: bfloat16 [16, 2048, 4096], P('section', 'expert'), may hold values from -6 to 6
- token_expert_choice: int32 [16, 2048, 8], P('section', 'expert'), may hold values from 0 to 127, as said below
- route_gate_steps: int32 [16, 2048, 8], P('section', 'expert'), may hold values from 1 to 4096
- gate_weight: bfloat16 [16, 4096, 4096], P('section', 'expert'), may hold values from -0.09375 to 0.09375
- up_weight: bfloat16 [16, 4096, 4096], P('section', 'expert'), may hold values from -0.09375 to 0.09375
- down_weight: bfloat16 [16, 4096, 4096], P('section', 'expert'), may hold values from -0.1875 to 0.1875
- adapter_down_maps: bfloat16 [16, 4096, 16], P('section', 'expert'), may hold values from -0.1875 to 0.1875
- adapter_up_maps: bfloat16 [16, 4, 16, 4096], P('section'), may hold values from -1.5 to 1.5
- cotangent: bfloat16 [16, 2048, 4096], P('section', 'expert'), may hold values from -6 to 6
Outputs:
- next_input: bfloat16 [16, 2048, 4096], P('section', 'expert')
- prev_grad: bfloat16 [16, 2048, 4096], P('section', 'expert')
- adapter_a_grad: float32 [16, 4096, 16], P('section', 'expert')
- adapter_b_grad: float32 [16, 4, 16, 4096], P('section', None, None, 'expert')
The draws below stay inside these ranges and needn't reach their ends.
Inputs may be any that keep to these rules, and one draw needn't show every extreme that they name: `token_expert_choice`: every token names 8 different experts. The experts below 4 are those in flight; the tokens of one device (aligned blocks of 128 tokens of a section) name any one of them at most 16 times, and in every section one of them is named exactly 16 times by the tokens of every device.
All inputs are finite; a program needn't handle non-finite values.
Results may differ from the reference program's by a relative error of at most 0.0069.
Values may be sent and summed in bfloat16 or wider, within the bound.
A program may use at most 64 MiB of HBM per device.

```python
import jax
import jax.numpy as jnp
from jax import lax

MODEL_DIM = 4096
TOP = 8
ADAPTER_RANK = 16
SPLIT = 4
HID_DEV = 256
TOK_DEV = 128
EXPERTS = 128
ACTIVE_EXPERTS = 4
EXPERT_HIDDEN = 1024
ACTIVE_UNITS = 4096
MOST = 16
TOKENS = 2048
N_SECTION = 16
N_EXPERT = 16


def draw_token_expert_choice(key, part):
    key = jax.random.fold_in(key, 11)
    subkeys = jax.random.split(key, 6)
    outer_pool = EXPERTS - ACTIVE_EXPERTS
    stride = outer_pool // TOP
    busiest = jax.random.randint(subkeys[0], (N_SECTION, 1, 1), 0, ACTIVE_EXPERTS)
    ceiling = jax.random.randint(subkeys[1], (N_SECTION, 1, ACTIVE_EXPERTS), max(MOST // 8, 1), max(MOST // 2, 1) + 1)
    counts = jax.random.randint(subkeys[2], (N_SECTION, N_EXPERT, ACTIVE_EXPERTS), 0, 1 << 20) % ceiling + 1
    flight_ids = jnp.arange(ACTIVE_EXPERTS, dtype=jnp.int32)
    counts = jnp.where(flight_ids[None, None, :] == busiest, MOST, counts)
    scores = jax.random.randint(subkeys[3], (N_SECTION, N_EXPERT, ACTIVE_EXPERTS, TOK_DEV), 0, 1 << 20) * TOK_DEV
    scores = scores + jnp.arange(TOK_DEV, dtype=jnp.int32)
    token_rank = jnp.argsort(jnp.argsort(scores, axis=-1), axis=-1)
    picked = (token_rank < counts[..., None]).astype(jnp.int32)
    picked = jnp.transpose(picked, (0, 1, 3, 2))
    taken_count = picked.sum(-1)
    position = jnp.cumsum(picked, axis=-1) - picked
    route_pos = jnp.arange(TOP, dtype=jnp.int32)
    inside = (picked[..., None] * (position[..., None] == route_pos).astype(jnp.int32) * flight_ids[:, None]).sum(-2)
    start_id = jax.random.randint(subkeys[4], (N_SECTION, N_EXPERT, TOK_DEV, 1), 0, outer_pool)
    outside = ACTIVE_EXPERTS + (start_id + route_pos * stride) % outer_pool
    ordered = jnp.where(route_pos < taken_count[..., None], inside, outside)
    rotation = jax.random.randint(subkeys[5], (N_SECTION, N_EXPERT, TOK_DEV, 1), 0, TOP)
    ordered = jnp.take_along_axis(ordered, (route_pos + rotation) % TOP, axis=-1)
    return ordered.reshape(N_SECTION, TOKENS, TOP).astype(jnp.int32)


def with_ends(result, stream_key, smallest, high):
    dims = result.shape
    place = [jax.random.randint(jax.random.fold_in(stream_key, axis), (), 0, dims[axis]) for axis in range(len(dims))]
    result = result.at[tuple(place)].set(smallest)
    longest = dims.index(max(dims))
    place[longest] = (place[longest] + 1) % dims[longest]
    return result.at[tuple(place)].set(high)


def block_scale(stream_key, extent, cuts, least, top_value):
    def one(dim, blocks):
        heights = jax.random.uniform(jax.random.fold_in(jax.random.fold_in(stream_key, 6), dim), (blocks,), jnp.float32, least / len(cuts), top_value / len(cuts))
        return jnp.repeat(jnp.exp(heights), extent[dim] // blocks).reshape((-1,) + (1,) * (len(extent) - dim - 1))

    loudness = one(*cuts[0])
    for cut in cuts[1:]:
        loudness = loudness * one(*cut)
    return loudness


def centred(rng, shape, width, reach, shards=(), kind=jnp.bfloat16):
    drawn = jax.random.normal(rng, shape, jnp.float32) * width
    if len(shards) > 0:
        drawn = block_scale(rng, shape, shards, -0.22, 0.18) * drawn
    return jnp.clip(drawn, min=-reach, max=reach).astype(kind)


def setup_inputs(seed: int = 0) -> dict:
    keys = jax.random.split(jax.random.key(seed), 10)
    section_layer_input = centred(keys[0], (N_SECTION, TOKENS, MODEL_DIM), 1.0, 6.0, ((0, 16), (1, 16)))
    token_expert_choice = draw_token_expert_choice(jax.random.fold_in(keys[9], 71), 0)
    route_gate_steps = with_ends(jax.random.randint(keys[2], (N_SECTION, TOKENS, TOP), 1, 4097), jax.random.fold_in(keys[2], 1), 1, 4096).astype(jnp.int32)
    gate_weight = centred(keys[3], (N_SECTION, ACTIVE_UNITS, MODEL_DIM), MODEL_DIM ** -0.5, 0.09375, ((0, 16), (1, 16)))
    up_weight = centred(keys[4], (N_SECTION, ACTIVE_UNITS, MODEL_DIM), MODEL_DIM ** -0.5, 0.09375, ((0, 16), (1, 16)))
    down_weight = centred(keys[5], (N_SECTION, ACTIVE_UNITS, MODEL_DIM), EXPERT_HIDDEN ** -0.5, 0.1875, ((0, 16), (1, 16)))
    adapter_down_maps = centred(keys[6], (N_SECTION, ACTIVE_UNITS, ADAPTER_RANK), EXPERT_HIDDEN ** -0.5, 0.1875, ((0, 16), (1, 16)))
    adapter_up_maps = centred(keys[7], (N_SECTION, ACTIVE_EXPERTS, ADAPTER_RANK, MODEL_DIM), ADAPTER_RANK ** -0.5, 1.5, ((0, 16),))
    cotangent = centred(keys[8], (N_SECTION, TOKENS, MODEL_DIM), 1.0, 6.0, ((0, 16), (1, 16)))
    return dict(section_layer_input=section_layer_input, token_expert_choice=token_expert_choice, route_gate_steps=route_gate_steps, gate_weight=gate_weight, up_weight=up_weight, down_weight=down_weight, adapter_down_maps=adapter_down_maps, adapter_up_maps=adapter_up_maps, cotangent=cotangent)


LOWRANK_SCALE = 2.0
LEVEL_STEP = 1.0 / 4096.0


def expert_forward(in_rows, gate_proj, up_proj, down_proj, down_adapter_factor, up_adapter_factor):
    contract_last = (((1,), (1,)), ((), ()))
    pre_gate = lax.dot_general(in_rows, gate_proj, contract_last, preferred_element_type=jnp.float32)
    pre_up = lax.dot_general(in_rows, up_proj, contract_last, preferred_element_type=jnp.float32)
    hidden = (jax.nn.silu(pre_gate) * pre_up).astype(jnp.bfloat16)
    projected_hidden = jnp.dot(hidden, down_adapter_factor, preferred_element_type=jnp.float32).astype(jnp.bfloat16)
    layer_result_rows = jnp.dot(hidden, down_proj, preferred_element_type=jnp.float32)
    layer_result_rows = (layer_result_rows + LOWRANK_SCALE * jnp.dot(projected_hidden, up_adapter_factor, preferred_element_type=jnp.float32)).astype(jnp.bfloat16)
    return pre_gate, pre_up, hidden, projected_hidden, layer_result_rows


def expert_backward(grad_in_rows, pre_gate, pre_up, gate_proj, up_proj, down_proj, down_adapter_factor, up_adapter_factor):
    contract_last = (((1,), (1,)), ((), ()))
    adapter_product = lax.dot_general(grad_in_rows, up_adapter_factor, contract_last, preferred_element_type=jnp.float32)
    adapter_product = (LOWRANK_SCALE * adapter_product).astype(jnp.bfloat16)
    grad_hidden = lax.dot_general(grad_in_rows, down_proj, contract_last, preferred_element_type=jnp.float32)
    grad_hidden = grad_hidden + lax.dot_general(adapter_product, down_adapter_factor, contract_last, preferred_element_type=jnp.float32)
    sigmoid_gate = jax.nn.sigmoid(pre_gate)
    grad_gate = (grad_hidden * pre_up * sigmoid_gate * (1.0 + pre_gate * (1.0 - sigmoid_gate))).astype(jnp.bfloat16)
    grad_up = (grad_hidden * pre_gate * sigmoid_gate).astype(jnp.bfloat16)
    grad_input = jnp.dot(grad_gate, gate_proj, preferred_element_type=jnp.float32)
    grad_input = (grad_input + jnp.dot(grad_up, up_proj, preferred_element_type=jnp.float32)).astype(jnp.bfloat16)
    return adapter_product, grad_input


def section_sweep(operands):
    tokens, route_ids, levels, gate_all, up_all, down_all, adapter_a_all, adapter_b_all, upstream = operands
    window_units = HID_DEV * SPLIT
    reduce_over_rows = (((0,), (0,)), ((), ()))
    block_ids = route_ids.reshape(N_EXPERT, TOK_DEV, TOP)
    block_levels = levels.reshape(N_EXPERT, TOK_DEV, TOP)
    offsets = (jnp.arange(N_EXPERT, dtype=jnp.int32)[:, None] * TOK_DEV
               + jnp.arange(TOK_DEV, dtype=jnp.int32)[None, :])
    out_sum = jnp.zeros((TOKENS, MODEL_DIM), jnp.float32)
    grad_sum = jnp.zeros((TOKENS, MODEL_DIM), jnp.float32)
    a_grads = []
    b_grads = []
    for expert in range(ACTIVE_EXPERTS):
        onehot = (block_ids == expert).astype(jnp.int32)
        routed = onehot.sum(-1)
        weight = (onehot * block_levels).sum(-1).astype(jnp.float32) * LEVEL_STEP
        slot_index = jnp.cumsum(routed, axis=1) - routed
        placement = ((slot_index[..., None] == jnp.arange(MOST, dtype=jnp.int32))
                     & (routed[..., None] > 0)).astype(jnp.int32)
        row_index = (placement * offsets[..., None]).sum(1).reshape(-1).astype(jnp.int32)
        is_valid = placement.sum(1).reshape(-1) > 0
        slot_gate = (placement.astype(jnp.float32) * weight[..., None]).sum(1).reshape(-1)
        token_rows = jnp.where(is_valid[:, None], tokens[row_index], jnp.zeros((), jnp.bfloat16))
        gated = (upstream[row_index].astype(jnp.float32) * slot_gate[:, None]).astype(jnp.bfloat16)
        gradient_rows_local = jnp.where(is_valid[:, None], gated, jnp.zeros((), jnp.bfloat16))
        out_rows = jnp.zeros((N_EXPERT * MOST, MODEL_DIM), jnp.float32)
        back_rows = jnp.zeros((N_EXPERT * MOST, MODEL_DIM), jnp.float32)
        up_factor_gradient = jnp.zeros((ADAPTER_RANK, MODEL_DIM), jnp.float32)
        for quarter in range(SPLIT):
            unit_start = expert * window_units + quarter * HID_DEV
            gate_proj = gate_all[unit_start:unit_start + HID_DEV]
            up_proj = up_all[unit_start:unit_start + HID_DEV]
            down_proj = down_all[unit_start:unit_start + HID_DEV]
            down_adapter_factor = adapter_a_all[unit_start:unit_start + HID_DEV]
            up_adapter_factor = adapter_b_all[expert]
            pre_gate, pre_up, hidden, projected_hidden, layer_result_rows = expert_forward(
                token_rows, gate_proj, up_proj, down_proj, down_adapter_factor, up_adapter_factor)
            adapter_product, grad_input = expert_backward(
                gradient_rows_local, pre_gate, pre_up, gate_proj, up_proj, down_proj, down_adapter_factor, up_adapter_factor)
            out_rows = out_rows + layer_result_rows.astype(jnp.float32)
            back_rows = back_rows + grad_input.astype(jnp.float32)
            a_grads.append(lax.dot_general(hidden, adapter_product, reduce_over_rows, preferred_element_type=jnp.float32))
            up_factor_gradient = up_factor_gradient + LOWRANK_SCALE * lax.dot_general(projected_hidden, gradient_rows_local, reduce_over_rows,
                                                          preferred_element_type=jnp.float32)
        out_sum = out_sum.at[row_index].add(slot_gate[:, None] * out_rows)
        grad_sum = grad_sum.at[row_index].add(back_rows)
        b_grads.append(up_factor_gradient)
    return (out_sum.astype(jnp.bfloat16), grad_sum.astype(jnp.bfloat16),
            jnp.concatenate(a_grads, axis=0), jnp.stack(b_grads, axis=0))


def reference(section_layer_input, token_expert_choice, route_gate_steps, gate_weight, up_weight, down_weight, adapter_down_maps, adapter_up_maps, cotangent):
    moe_out, layer_grad, a_grad, up_factor_gradient = lax.map(
        section_sweep, (section_layer_input, token_expert_choice, route_gate_steps, gate_weight, up_weight, down_weight, adapter_down_maps, adapter_up_maps, cotangent))
    return (jnp.roll(moe_out, 1, axis=0), jnp.roll(layer_grad, -1, axis=0), a_grad, up_factor_gradient)
```

```python
import functools

import jax
import jax.numpy as jnp
from jax import lax
from jax.experimental import pallas as pl
from jax.experimental.pallas import tpu as pltpu
from jax.sharding import PartitionSpec as P

SPLIT = 4
MOST = 16
LOWRANK_SCALE = 2.0
LEVEL_STEP = 1.0 / 4096.0
F32 = jnp.float32
BF16 = jnp.bfloat16
FWD, BWD = 0, 1
LEFT, RIGHT = 0, 1


def dot_nt(a, b):
    return lax.dot_general(a, b, (((1,), (1,)), ((), ())), preferred_element_type=F32)


def dot_nn(a, b):
    return jnp.dot(a, b, preferred_element_type=F32)


def kernel(
    choice_ref, steps_ref, at_ref, tok_hbm, cot_hbm, wg_hbm, wu_hbm, wd_hbm, bup_hbm,
    out_hbm, grad_hbm, bg_hbm, ag_ref,
    rows_v, wg, wu, wd, bup, send, recv, pre_gate_v, pre_up_v, hid_v, lr_v,
    part, from_a, sum_b, from_b, fin, back, mix, mix_in, lat, lat_in, bsend, bg_v, out_v,
    load_sem, y_s, y_r, x1_s, x1_r, x2_s, x2_r, a_s, a_r, b_s, b_r, c_s, c_r,
    mix_s, mix_r, lat_s, lat_r, bg_s, bg_r, out_sem,
):
    half = recv.shape[-1]
    units = wg.shape[0]
    tokens = rows_v.shape[1]
    n_section = lax.axis_size("section")
    s = lax.axis_index("section")
    me = lax.axis_index("expert")
    y, x = me // SPLIT, me % SPLIT
    xr, xo, xl = (x + 1) % SPLIT, (x + 2) % SPLIT, (x + 3) % SPLIT
    s_next, s_prev = (s + 1) % n_section, (s + n_section - 1) % n_section

    def dev(row, col, sec=s):
        return {"section": sec, "expert": row * SPLIT + col}

    beside = (dev(y, xl), dev(y, xr))
    toward = (s_next, s_prev)

    def copy(src, dst, send_sem, recv_sem, device):
        return pltpu.make_async_remote_copy(
            src_ref=src, dst_ref=dst, send_sem=send_sem, recv_sem=recv_sem,
            device_id=device, device_id_type=pl.DeviceIdType.MESH,
        )

    def loop(first, last, body):
        def step(k, _):
            body(k)
            return 0
        lax.fori_loop(first, last, step, 0)

    loads = [
        pltpu.make_async_copy(src, dst, load_sem.at[i])
        for i, (src, dst) in enumerate((
            (tok_hbm, rows_v.at[FWD]), (cot_hbm, rows_v.at[BWD]), (wg_hbm, wg), (wu_hbm, wu),
            (wd_hbm, wd), (bup_hbm.at[y], bup),
        ))
    ]
    for load in loads:
        load.start()

    barrier = pltpu.get_barrier_semaphore()
    partners = [dev(y, xl), dev(y, xr), dev(y, xo)]
    partners += [dev((y + k) % SPLIT, x) for k in range(1, SPLIT)]
    partners += [dev((y + k) % SPLIT, x, sec) for k in range(SPLIT) for sec in toward]
    for device in partners:
        pl.semaphore_signal(barrier, inc=1, device_id=device, device_id_type=pl.DeviceIdType.MESH)

    shape = (SPLIT * MOST, tokens)
    row = lax.broadcasted_iota(jnp.int32, shape, 0)
    slot = row % MOST
    expert = (y + SPLIT - row // MOST) % SPLIT
    choice, steps = choice_ref[...], steps_ref[...]
    routed = jnp.zeros(shape, jnp.int32)
    gate = jnp.zeros(shape, jnp.int32)
    for j in range(choice.shape[0]):
        hit = choice[j:j + 1, :] == expert
        routed = jnp.where(hit, 1, routed)
        gate = jnp.where(hit, steps[j:j + 1, :], gate)
    square = (tokens, tokens)
    earlier = lax.broadcasted_iota(jnp.int32, square, 0) < lax.broadcasted_iota(jnp.int32, square, 1)
    taken = dot_nn(routed.astype(F32).astype(BF16), earlier.astype(F32).astype(BF16))
    placed = (routed > 0) & (taken == slot.astype(F32))
    place = jnp.where(placed, 1.0, 0.0).astype(F32)
    weight = place * (gate.astype(F32) * LEVEL_STEP)
    slot_gate = jnp.sum(weight, axis=1, keepdims=True)
    place_half = place.astype(BF16)

    def dispatch(ph):
        for h in range(2):
            out = dot_nn(place_half, rows_v[ph, :, h * half:(h + 1) * half])
            if ph == BWD:
                out = out * slot_gate
            out = out.astype(BF16)
            recv[ph, 0, h, pl.ds(x, 1)] = out[:MOST][None]
            for k in range(1, SPLIT):
                send[ph, k, h] = out[k * MOST:(k + 1) * MOST]

    def y_copy(ph, k, h):
        return copy(send.at[ph, k, h], recv.at[ph, k, h, x], y_s.at[ph, k, h], y_r.at[ph, k, h],
                    dev((y + SPLIT - k) % SPLIT, x))

    def x1_copy(ph, k, way, h, col):
        return copy(recv.at[ph, k, h, col], recv.at[ph, k, h, col], x1_s.at[ph, k, way, h],
                    x1_r.at[ph, k, way, h], beside[way])

    def x2_copy(ph, k, way, col):
        return copy(recv.at[ph, k, way, col], recv.at[ph, k, way, col], x2_s.at[ph, k, way],
                    x2_r.at[ph, k, way], beside[way])

    def x1_start(ph, k):
        for first in range(2):
            x1_copy(ph, k, LEFT, first, x).start()
            x1_copy(ph, k, RIGHT, 1 - first, x).start()

    def x2_start(ph, k):
        x1_copy(ph, k, LEFT, 0, xr).wait_recv()
        x2_copy(ph, k, LEFT, xr).start()
        x1_copy(ph, k, RIGHT, 1, xl).wait_recv()
        x2_copy(ph, k, RIGHT, xl).start()

    def gathered(ph, k):
        x1_copy(ph, k, LEFT, 1, xr).wait_recv()
        x1_copy(ph, k, RIGHT, 0, xl).wait_recv()
        x2_copy(ph, k, LEFT, xo).wait_recv()
        x2_copy(ph, k, RIGHT, xo).wait_recv()

    def y_wait(ph, k):
        for h in range(2):
            y_copy(ph, k, h).wait_recv()
        x1_start(ph, k)

    def a_copy(ph, k, way):
        return copy(part.at[ph, k, way, xo], from_a.at[ph, k, way], a_s.at[ph, k, way],
                    a_r.at[ph, k, way], beside[way])

    def b_copy(ph, k, way, late):
        src = sum_b.at[ph, k, way] if late else part.at[ph, k, 1 - way, (xl, xr)[way]]
        h = way if late else 1 - way
        return copy(src, from_b.at[ph, k, way, h], b_s.at[ph, k, way, h], b_r.at[ph, k, way, h],
                    beside[way])

    def parts_start(ph, k):
        for way in (LEFT, RIGHT):
            a_copy(ph, k, way).start()
        for way in (LEFT, RIGHT):
            b_copy(ph, k, way, False).start()

    def relay(ph, k):
        for way in (LEFT, RIGHT):
            a_copy(ph, k, way).wait_recv()
            mine = part[ph, k, way, pl.ds((xl, xr)[way], 1)][0].astype(F32)
            sum_b[ph, k, way] = (mine + from_a[ph, k, way].astype(F32)).astype(BF16)
            b_copy(ph, k, way, True).start()

    def c_copy(ph, k):
        return copy(fin.at[ph, k], back.at[ph, k], c_s.at[ph, k], c_r.at[ph, k],
                    dev((y + k) % SPLIT, x, toward[ph]))

    def finish(ph, k):
        for way in (LEFT, RIGHT):
            for late in (False, True):
                b_copy(ph, k, way, late).wait_recv()
        for h in range(2):
            total = part[ph, k, h, pl.ds(x, 1)][0].astype(F32)
            total = total + from_b[ph, k, LEFT, h].astype(F32) + from_b[ph, k, RIGHT, h].astype(F32)
            fin[ph, k, h] = total.astype(BF16)
        c_copy(ph, k).start()

    def rows_of(ph, k, h):
        return recv[ph, k, h].reshape(SPLIT * MOST, half)

    def forward(k):
        pre_gate = dot_nt(rows_of(FWD, k, 0), wg[:, :half]) + dot_nt(rows_of(FWD, k, 1), wg[:, half:])
        pre_up = dot_nt(rows_of(FWD, k, 0), wu[:, :half]) + dot_nt(rows_of(FWD, k, 1), wu[:, half:])
        hidden = (pre_gate * jax.nn.sigmoid(pre_gate) * pre_up).astype(BF16)
        pre_gate_v[k] = pre_gate
        pre_up_v[k] = pre_up
        hid_v[k] = hidden
        latent = dot_nt(hidden, at_ref[...]).astype(BF16)
        latent = (LOWRANK_SCALE * latent.astype(F32)).astype(BF16)
        for h in range(2):
            cols = slice(h * half, (h + 1) * half)
            out = dot_nn(hidden, wd[:, cols]) + dot_nn(latent, bup[:, cols])
            part[FWD, k, h] = out.astype(BF16).reshape(SPLIT, MOST, half)

    def backward(k):
        low = dot_nt(rows_of(BWD, k, 0), bup[:, :half]) + dot_nt(rows_of(BWD, k, 1), bup[:, half:])
        low = (LOWRANK_SCALE * low).astype(BF16)
        lr_v[k] = low
        grad_hidden = dot_nt(rows_of(BWD, k, 0), wd[:, :half]) + dot_nt(rows_of(BWD, k, 1), wd[:, half:])
        grad_hidden = grad_hidden + dot_nn(low, at_ref[...])
        pre_gate, pre_up = pre_gate_v[k], pre_up_v[k]
        sig = jax.nn.sigmoid(pre_gate)
        grad_gate = (grad_hidden * pre_up * sig * (1.0 + pre_gate * (1.0 - sig))).astype(BF16)
        grad_up = (grad_hidden * pre_gate * sig).astype(BF16)
        for h in range(2):
            cols = slice(h * half, (h + 1) * half)
            out = dot_nn(grad_gate, wg[:, cols]) + dot_nn(grad_up, wu[:, cols])
            part[BWD, k, h] = out.astype(BF16).reshape(SPLIT, MOST, half)

    loads[0].wait()
    dispatch(FWD)
    pl.semaphore_wait(barrier, len(partners))
    x1_start(FWD, 0)
    for k in (1, 3, 2):
        for h in range(2):
            y_copy(FWD, k, h).start()

    loads[1].wait()
    dispatch(BWD)
    x1_start(BWD, 0)
    for k in (1, 3, 2):
        for h in range(2):
            y_copy(BWD, k, h).start()

    high = weight.astype(BF16).astype(F32)
    mixes = (jnp.concatenate([high, weight - high], axis=0),
             jnp.concatenate([place, jnp.zeros_like(place)], axis=0))
    for ph in (FWD, BWD):
        mix[ph] = jnp.transpose(mixes[ph]).astype(BF16)

    def mix_copy(ph):
        return copy(mix.at[ph], mix_in.at[ph], mix_s.at[ph], mix_r.at[ph], dev(y, x, toward[ph]))

    for ph in (FWD, BWD):
        mix_copy(ph).start()

    loop(1, SPLIT, lambda k: y_wait(FWD, k))
    loop(1, SPLIT, lambda k: y_wait(BWD, k))
    loop(0, SPLIT, lambda k: x2_start(FWD, k))
    for load in loads[2:]:
        load.wait()

    def forward_step(k):
        gathered(FWD, k)
        forward(k)
        parts_start(FWD, k)
        x2_start(BWD, k)

    loop(0, SPLIT, forward_step)

    hidden_all = hid_v[...].reshape(SPLIT * SPLIT * MOST, units)
    lat[...] = dot_nt(at_ref[...], hidden_all).astype(BF16)

    def lat_copy(i):
        return copy(lat, lat_in.at[i], lat_s.at[i], lat_r.at[i],
                    (dev(y, xl), dev(y, xr), dev(y, xo))[i])

    for i in range(3):
        lat_copy(i).start()

    def backward_step(k):
        gathered(BWD, k)
        backward(k)
        parts_start(BWD, k)
        relay(FWD, k)

    loop(0, SPLIT, backward_step)

    ag_ref[...] = lax.dot_general(
        lr_v[...].reshape(SPLIT * SPLIT * MOST, lr_v.shape[-1]),
        hid_v[...].reshape(SPLIT * SPLIT * MOST, units),
        (((0,), (0,)), ((), ())), preferred_element_type=F32)

    def middle_step(k):
        relay(BWD, k)
        finish(FWD, k)

    loop(0, SPLIT, middle_step)

    width = bg_v.shape[-1]
    lat_sum = lat[...].astype(F32)
    for i in range(3):
        lat_copy(i).wait_recv()
        lat_sum = lat_sum + lat_in[i].astype(F32)
    lat_sum = LOWRANK_SCALE * lat_sum
    lat_high = lat_sum.astype(BF16)
    lat_low = (lat_sum - lat_high.astype(F32)).astype(BF16)

    def bg_copy(k):
        return copy(bsend.at[k], bg_v.at[y], bg_s.at[k], bg_r.at[k], dev((y + k) % SPLIT, x))

    def bg_wait(k):
        return copy(bsend.at[k], bg_v.at[(y + SPLIT - k) % SPLIT], bg_s.at[k], bg_r.at[k],
                    dev((y + k) % SPLIT, x))

    per_half = half // width
    for k in range(SPLIT):
        block = ((y + k) % SPLIT) * SPLIT + x
        cols = pl.ds(pl.multiple_of((block % per_half) * width, width), width)
        grad_rows = recv[BWD, :, pl.ds(block // per_half, 1), :, :, cols]
        grad_rows = grad_rows.reshape(SPLIT * SPLIT * MOST, width)
        value = dot_nn(lat_high, grad_rows) + dot_nn(lat_low, grad_rows)
        if k == 0:
            bg_v[pl.ds(y, 1)] = value[None]
        else:
            bsend[k] = value
            bg_copy(k).start()

    tile = min(512, half)

    def out_copy(ph, h, n):
        cols = slice(h * half + n * tile, h * half + (n + 1) * tile)
        return pltpu.make_async_copy(
            out_v.at[ph, :, cols], (out_hbm, grad_hbm)[ph].at[:, cols],
            out_sem.at[ph, h * (half // tile) + n])

    def combine(ph):
        mix_copy(ph).wait_recv()
        for k in range(SPLIT):
            c_copy(ph, k).wait_recv()
        spread = mix_in[ph]
        for h in range(2):
            for n in range(half // tile):
                block = back[ph, :, h, :, n * tile:(n + 1) * tile].reshape(SPLIT * MOST, tile)
                block = jnp.concatenate([block, block], axis=0)
                cols = slice(h * half + n * tile, h * half + (n + 1) * tile)
                out_v[ph, :, cols] = dot_nn(spread, block).astype(BF16)
                out_copy(ph, h, n).start()

    loop(0, SPLIT - 1, lambda k: finish(BWD, k))
    combine(FWD)
    finish(BWD, SPLIT - 1)
    for k in range(1, SPLIT):
        bg_wait(k).wait_recv()
    bg_out = pltpu.make_async_copy(bg_v, bg_hbm, load_sem.at[0])
    bg_out.start()
    combine(BWD)

    bg_out.wait()
    for ph in (FWD, BWD):
        mix_copy(ph).wait_send()
    for i in range(3):
        lat_copy(i).wait_send()
    for k in range(1, SPLIT):
        bg_copy(k).wait_send()

    def sent(k):
        for ph in (FWD, BWD):
            for way in (LEFT, RIGHT):
                for h in range(2):
                    x1_copy(ph, k, way, h, x).wait_send()
                    b_copy(ph, k, way, h == way).wait_send()
                x2_copy(ph, k, way, x).wait_send()
                a_copy(ph, k, way).wait_send()
            c_copy(ph, k).wait_send()

    loop(0, SPLIT, sent)

    def y_sent(k):
        for ph in (FWD, BWD):
            for h in range(2):
                y_copy(ph, k, h).wait_send()

    loop(1, SPLIT, y_sent)
    for ph in (FWD, BWD):
        for h in range(2):
            for n in range(half // tile):
                out_copy(ph, h, n).wait()


def on_device(
    section_layer_input, token_expert_choice, route_gate_steps, gate_weight, up_weight, down_weight,
    adapter_down_maps, adapter_up_maps, cotangent,
):
    tokens, width = section_layer_input.shape[1:]
    units = gate_weight.shape[1]
    rank = adapter_down_maps.shape[2]
    half = width // 2
    cols = width // lax.axis_size("expert")
    dma = pltpu.SemaphoreType.DMA
    flight = SPLIT * MOST
    tile = min(512, half)
    anywhere = pl.BlockSpec(memory_space=pl.ANY)
    vmem = pl.BlockSpec(memory_space=pltpu.VMEM)
    out, grad, b_grad, a_grad = pl.pallas_call(
        kernel,
        out_shape=(
            jax.ShapeDtypeStruct((tokens, width), BF16),
            jax.ShapeDtypeStruct((tokens, width), BF16),
            jax.ShapeDtypeStruct((SPLIT, rank, cols), F32),
            jax.ShapeDtypeStruct((rank, units), F32),
        ),
        in_specs=[vmem] * 3 + [anywhere] * 6,
        out_specs=(anywhere, anywhere, anywhere, vmem),
        scratch_shapes=[
            pltpu.VMEM((2, tokens, width), BF16),
            pltpu.VMEM((units, width), BF16),
            pltpu.VMEM((units, width), BF16),
            pltpu.VMEM((units, width), BF16),
            pltpu.VMEM((rank, width), BF16),
            pltpu.VMEM((2, SPLIT, 2, MOST, half), BF16),
            pltpu.VMEM((2, SPLIT, 2, SPLIT, MOST, half), BF16),
            pltpu.VMEM((SPLIT, flight, units), F32),
            pltpu.VMEM((SPLIT, flight, units), F32),
            pltpu.VMEM((SPLIT, flight, units), BF16),
            pltpu.VMEM((SPLIT, flight, rank), BF16),
            pltpu.VMEM((2, SPLIT, 2, SPLIT, MOST, half), BF16),
            pltpu.VMEM((2, SPLIT, 2, MOST, half), BF16),
            pltpu.VMEM((2, SPLIT, 2, MOST, half), BF16),
            pltpu.VMEM((2, SPLIT, 2, 2, MOST, half), BF16),
            pltpu.VMEM((2, SPLIT, 2, MOST, half), BF16),
            pltpu.VMEM((2, SPLIT, 2, MOST, half), BF16),
            pltpu.VMEM((2, tokens, 2 * flight), BF16),
            pltpu.VMEM((2, tokens, 2 * flight), BF16),
            pltpu.VMEM((rank, SPLIT * flight), BF16),
            pltpu.VMEM((3, rank, SPLIT * flight), BF16),
            pltpu.VMEM((SPLIT, rank, cols), F32),
            pltpu.VMEM((SPLIT, rank, cols), F32),
            pltpu.VMEM((2, tokens, width), BF16),
            dma((6,)),
            dma((2, SPLIT, 2)), dma((2, SPLIT, 2)),
            dma((2, SPLIT, 2, 2)), dma((2, SPLIT, 2, 2)),
            dma((2, SPLIT, 2)), dma((2, SPLIT, 2)),
            dma((2, SPLIT, 2)), dma((2, SPLIT, 2)),
            dma((2, SPLIT, 2, 2)), dma((2, SPLIT, 2, 2)),
            dma((2, SPLIT)), dma((2, SPLIT)),
            dma((2,)), dma((2,)),
            dma((3,)), dma((3,)),
            dma((SPLIT,)), dma((SPLIT,)),
            dma((2, 2 * (half // tile))),
        ],
        compiler_params=pltpu.CompilerParams(
            collective_id=0, has_side_effects=True, vmem_limit_bytes=48 * 1024 * 1024),
    )(
        token_expert_choice[0].T, route_gate_steps[0].T, adapter_down_maps[0].T,
        section_layer_input[0], cotangent[0], gate_weight[0], up_weight[0], down_weight[0],
        adapter_up_maps[0],
    )
    return out[None], grad[None], a_grad.T[None], b_grad[None]


def solution(mesh):
    tokens = P("section", "expert", None)
    return jax.shard_map(
        on_device,
        mesh=mesh,
        in_specs=(tokens,) * 7 + (P("section", None, None, None), tokens),
        out_specs=(tokens, tokens, tokens, P("section", None, None, "expert")),
        check_vma=False,
    )
```

```python
import functools

import jax
import jax.numpy as jnp
from jax import lax
from jax.experimental import pallas as pl
from jax.experimental.pallas import tpu as pltpu
from jax.sharding import PartitionSpec as P

SPLIT = 4
MOST = 16
LOWRANK_SCALE = 2.0
LEVEL_STEP = 1.0 / 4096.0
F32 = jnp.float32
BF16 = jnp.bfloat16
FWD, BWD = 0, 1
LEFT, RIGHT = 0, 1


def dot_nt(a, b):
    return lax.dot_general(a, b, (((1,), (1,)), ((), ())), preferred_element_type=F32)


def dot_nn(a, b):
    return jnp.dot(a, b, preferred_element_type=F32)


def kernel(
    choice_hbm, steps_hbm, at_hbm, tok_hbm, cot_hbm, wg_hbm, wu_hbm, wd_hbm, bup_hbm,
    out_v, back_g, mix_g, bg_v, ag_ref,
    rows_v, wg, wu, wd, bup, send, recv, pre_gate_v, pre_up_v, hid_v, lr_v,
    part, from_a, sum_b, from_b, fin, back_f, mix, mix_f, lat, lat_in, bsend, choice_v, steps_v, at_v,
    load_sem, y_s, y_r, x1_s, x1_r, x2_s, x2_r, a_s, a_r, b_s, b_r, c_s, c_r,
    mix_s, mix_r, lat_s, lat_r, bg_s, bg_r,
):
    half = recv.shape[-1]
    units = wg.shape[0]
    tokens = rows_v.shape[1]
    n_section = lax.axis_size("section")
    s = lax.axis_index("section")
    me = lax.axis_index("expert")
    y, x = me // SPLIT, me % SPLIT
    xr, xo, xl = (x + 1) % SPLIT, (x + 2) % SPLIT, (x + 3) % SPLIT
    s_next, s_prev = (s + 1) % n_section, (s + n_section - 1) % n_section

    def dev(row, col, sec=s):
        return {"section": sec, "expert": row * SPLIT + col}

    beside = (dev(y, xl), dev(y, xr))
    toward = (s_next, s_prev)

    def copy(src, dst, send_sem, recv_sem, device):
        return pltpu.make_async_remote_copy(
            src_ref=src, dst_ref=dst, send_sem=send_sem, recv_sem=recv_sem,
            device_id=device, device_id_type=pl.DeviceIdType.MESH,
        )

    def loop(first, last, body):
        def step(k, _):
            body(k)
            return 0
        lax.fori_loop(first, last, step, 0)

    loads = [
        pltpu.make_async_copy(src, dst, load_sem.at[i])
        for i, (src, dst) in enumerate((
            (choice_hbm, choice_v), (steps_hbm, steps_v), (tok_hbm, rows_v.at[FWD]),
            (cot_hbm, rows_v.at[BWD]), (at_hbm, at_v), (wg_hbm, wg), (wu_hbm, wu), (wd_hbm, wd),
            (bup_hbm.at[y], bup),
        ))
    ]
    for load in loads:
        load.start()

    barrier = pltpu.get_barrier_semaphore()
    partners = [dev(y, xl), dev(y, xr), dev(y, xo)]
    partners += [dev((y + k) % SPLIT, x) for k in range(1, SPLIT)]
    partners += [dev((y + k) % SPLIT, x, sec) for k in range(SPLIT) for sec in toward]
    for device in partners:
        pl.semaphore_signal(barrier, inc=1, device_id=device, device_id_type=pl.DeviceIdType.MESH)

    shape = (SPLIT * MOST, tokens)
    row = lax.broadcasted_iota(jnp.int32, shape, 0)
    slot = row % MOST
    expert = (y + SPLIT - row // MOST) % SPLIT
    loads[0].wait()
    loads[1].wait()
    choice, steps = choice_v[...], steps_v[...]
    routed = jnp.zeros(shape, jnp.int32)
    gate = jnp.zeros(shape, jnp.int32)
    for j in range(choice.shape[0]):
        hit = choice[j:j + 1, :] == expert
        routed = jnp.where(hit, 1, routed)
        gate = jnp.where(hit, steps[j:j + 1, :], gate)
    square = (tokens, tokens)
    earlier = lax.broadcasted_iota(jnp.int32, square, 0) < lax.broadcasted_iota(jnp.int32, square, 1)
    taken = dot_nn(routed.astype(F32).astype(BF16), earlier.astype(F32).astype(BF16))
    placed = (routed > 0) & (taken == slot.astype(F32))
    place = jnp.where(placed, 1.0, 0.0).astype(F32)
    weight = place * (gate.astype(F32) * LEVEL_STEP)
    slot_gate = jnp.sum(weight, axis=1, keepdims=True)
    place_half = place.astype(BF16)

    def dispatch(ph):
        for h in range(2):
            out = dot_nn(place_half, rows_v[ph, :, h * half:(h + 1) * half])
            if ph == BWD:
                out = out * slot_gate
            out = out.astype(BF16)
            recv[ph, 0, h, pl.ds(x, 1)] = out[:MOST][None]
            for k in range(1, SPLIT):
                send[ph, k, h] = out[k * MOST:(k + 1) * MOST]

    def y_copy(ph, k, h):
        return copy(send.at[ph, k, h], recv.at[ph, k, h, x], y_s.at[ph, k, h], y_r.at[ph, k, h],
                    dev((y + SPLIT - k) % SPLIT, x))

    def x1_copy(ph, k, way, h, col):
        return copy(recv.at[ph, k, h, col], recv.at[ph, k, h, col], x1_s.at[ph, k, way, h],
                    x1_r.at[ph, k, way, h], beside[way])

    def x2_copy(ph, k, way, col):
        return copy(recv.at[ph, k, way, col], recv.at[ph, k, way, col], x2_s.at[ph, k, way],
                    x2_r.at[ph, k, way], beside[way])

    def x1_start(ph, k):
        for first in range(2):
            x1_copy(ph, k, LEFT, first, x).start()
            x1_copy(ph, k, RIGHT, 1 - first, x).start()

    def x2_start(ph, k):
        x1_copy(ph, k, LEFT, 0, xr).wait_recv()
        x2_copy(ph, k, LEFT, xr).start()
        x1_copy(ph, k, RIGHT, 1, xl).wait_recv()
        x2_copy(ph, k, RIGHT, xl).start()

    def gathered(ph, k):
        x1_copy(ph, k, LEFT, 1, xr).wait_recv()
        x1_copy(ph, k, RIGHT, 0, xl).wait_recv()
        x2_copy(ph, k, LEFT, xo).wait_recv()
        x2_copy(ph, k, RIGHT, xo).wait_recv()

    def y_wait(ph, k):
        for h in range(2):
            y_copy(ph, k, h).wait_recv()
        x1_start(ph, k)

    def a_copy(ph, k, way):
        return copy(part.at[ph, k, way, xo], from_a.at[ph, k, way], a_s.at[ph, k, way],
                    a_r.at[ph, k, way], beside[way])

    def b_copy(ph, k, way, late):
        src = sum_b.at[ph, k, way] if late else part.at[ph, k, 1 - way, (xl, xr)[way]]
        h = way if late else 1 - way
        return copy(src, from_b.at[ph, k, way, h], b_s.at[ph, k, way, h], b_r.at[ph, k, way, h],
                    beside[way])

    def parts_start(ph, k):
        for way in (LEFT, RIGHT):
            a_copy(ph, k, way).start()
        for way in (LEFT, RIGHT):
            b_copy(ph, k, way, False).start()

    def relay(ph, k):
        for way in (LEFT, RIGHT):
            a_copy(ph, k, way).wait_recv()
            mine = part[ph, k, way, pl.ds((xl, xr)[way], 1)][0].astype(F32)
            sum_b[ph, k, way] = (mine + from_a[ph, k, way].astype(F32)).astype(BF16)
            b_copy(ph, k, way, True).start()

    def c_copy(ph, k):
        return copy(fin.at[ph, k], (back_f, back_g)[ph].at[k], c_s.at[ph, k], c_r.at[ph, k],
                    dev((y + k) % SPLIT, x, toward[ph]))

    def finish(ph, k):
        for way in (LEFT, RIGHT):
            for late in (False, True):
                b_copy(ph, k, way, late).wait_recv()
        for h in range(2):
            total = part[ph, k, h, pl.ds(x, 1)][0].astype(F32)
            total = total + from_b[ph, k, LEFT, h].astype(F32) + from_b[ph, k, RIGHT, h].astype(F32)
            fin[ph, k, h] = total.astype(BF16)
        c_copy(ph, k).start()

    def rows_of(ph, k, h):
        return recv[ph, k, h].reshape(SPLIT * MOST, half)

    def forward(k):
        pre_gate = dot_nt(rows_of(FWD, k, 0), wg[:, :half]) + dot_nt(rows_of(FWD, k, 1), wg[:, half:])
        pre_up = dot_nt(rows_of(FWD, k, 0), wu[:, :half]) + dot_nt(rows_of(FWD, k, 1), wu[:, half:])
        hidden = (pre_gate * jax.nn.sigmoid(pre_gate) * pre_up).astype(BF16)
        pre_gate_v[k] = pre_gate
        pre_up_v[k] = pre_up
        hid_v[k] = hidden
        latent = dot_nt(hidden, at_v[...]).astype(BF16)
        latent = (LOWRANK_SCALE * latent.astype(F32)).astype(BF16)
        for h in range(2):
            cols = slice(h * half, (h + 1) * half)
            out = dot_nn(hidden, wd[:, cols]) + dot_nn(latent, bup[:, cols])
            part[FWD, k, h] = out.astype(BF16).reshape(SPLIT, MOST, half)

    def backward(k):
        low = dot_nt(rows_of(BWD, k, 0), bup[:, :half]) + dot_nt(rows_of(BWD, k, 1), bup[:, half:])
        low = (LOWRANK_SCALE * low).astype(BF16)
        lr_v[k] = low
        grad_hidden = dot_nt(rows_of(BWD, k, 0), wd[:, :half]) + dot_nt(rows_of(BWD, k, 1), wd[:, half:])
        grad_hidden = grad_hidden + dot_nn(low, at_v[...])
        pre_gate, pre_up = pre_gate_v[k], pre_up_v[k]
        sig = jax.nn.sigmoid(pre_gate)
        grad_gate = (grad_hidden * pre_up * sig * (1.0 + pre_gate * (1.0 - sig))).astype(BF16)
        grad_up = (grad_hidden * pre_gate * sig).astype(BF16)
        for h in range(2):
            cols = slice(h * half, (h + 1) * half)
            out = dot_nn(grad_gate, wg[:, cols]) + dot_nn(grad_up, wu[:, cols])
            part[BWD, k, h] = out.astype(BF16).reshape(SPLIT, MOST, half)

    loads[2].wait()
    dispatch(FWD)
    pl.semaphore_wait(barrier, len(partners))
    x1_start(FWD, 0)
    for k in (1, 3, 2):
        for h in range(2):
            y_copy(FWD, k, h).start()

    loads[3].wait()
    dispatch(BWD)
    x1_start(BWD, 0)
    for k in (1, 3, 2):
        for h in range(2):
            y_copy(BWD, k, h).start()

    high = weight.astype(BF16).astype(F32)
    mixes = (jnp.concatenate([high, weight - high], axis=0),
             jnp.concatenate([place, jnp.zeros_like(place)], axis=0))
    for ph in (FWD, BWD):
        mix[ph] = jnp.transpose(mixes[ph]).astype(BF16)

    def mix_copy(ph):
        return copy(mix.at[ph], (mix_f, mix_g)[ph], mix_s.at[ph], mix_r.at[ph], dev(y, x, toward[ph]))

    for ph in (FWD, BWD):
        mix_copy(ph).start()

    loop(1, SPLIT, lambda k: y_wait(FWD, k))
    loop(1, SPLIT, lambda k: y_wait(BWD, k))
    loop(0, SPLIT, lambda k: x2_start(FWD, k))
    for load in loads[4:]:
        load.wait()

    def forward_step(k):
        gathered(FWD, k)
        forward(k)
        parts_start(FWD, k)
        x2_start(BWD, k)

    loop(0, SPLIT, forward_step)

    hidden_all = hid_v[...].reshape(SPLIT * SPLIT * MOST, units)
    lat[...] = dot_nt(at_v[...], hidden_all).astype(BF16)

    def lat_copy(i):
        return copy(lat, lat_in.at[i], lat_s.at[i], lat_r.at[i],
                    (dev(y, xl), dev(y, xr), dev(y, xo))[i])

    for i in range(3):
        lat_copy(i).start()

    def backward_step(k):
        gathered(BWD, k)
        backward(k)
        parts_start(BWD, k)
        relay(FWD, k)

    loop(0, SPLIT, backward_step)

    ag_ref[...] = lax.dot_general(
        lr_v[...].reshape(SPLIT * SPLIT * MOST, lr_v.shape[-1]),
        hid_v[...].reshape(SPLIT * SPLIT * MOST, units),
        (((0,), (0,)), ((), ())), preferred_element_type=F32)

    def middle_step(k):
        relay(BWD, k)
        finish(FWD, k)

    loop(0, SPLIT, middle_step)

    width = bg_v.shape[-1]
    lat_sum = lat[...].astype(F32)
    for i in range(3):
        lat_copy(i).wait_recv()
        lat_sum = lat_sum + lat_in[i].astype(F32)
    lat_sum = LOWRANK_SCALE * lat_sum
    lat_high = lat_sum.astype(BF16)
    lat_low = (lat_sum - lat_high.astype(F32)).astype(BF16)

    def bg_copy(k):
        return copy(bsend.at[k], bg_v.at[y], bg_s.at[k], bg_r.at[k], dev((y + k) % SPLIT, x))

    def bg_wait(k):
        return copy(bsend.at[k], bg_v.at[(y + SPLIT - k) % SPLIT], bg_s.at[k], bg_r.at[k],
                    dev((y + k) % SPLIT, x))

    per_half = half // width
    for k in range(SPLIT):
        block = ((y + k) % SPLIT) * SPLIT + x
        cols = pl.ds(pl.multiple_of((block % per_half) * width, width), width)
        grad_rows = recv[BWD, :, pl.ds(block // per_half, 1), :, :, cols]
        grad_rows = grad_rows.reshape(SPLIT * SPLIT * MOST, width)
        value = dot_nn(lat_high, grad_rows) + dot_nn(lat_low, grad_rows)
        if k == 0:
            bg_v[pl.ds(y, 1)] = value[None]
        else:
            bsend[k] = value
            bg_copy(k).start()

    def arrived(ph):
        mix_copy(ph).wait_recv()
        for k in range(SPLIT):
            c_copy(ph, k).wait_recv()

    loop(0, SPLIT - 1, lambda k: finish(BWD, k))
    arrived(FWD)
    for cols, value in spread(mix_f, back_f):
        out_v[:, cols] = value
    finish(BWD, SPLIT - 1)
    for k in range(1, SPLIT):
        bg_wait(k).wait_recv()
    arrived(BWD)

    for ph in (FWD, BWD):
        mix_copy(ph).wait_send()
    for i in range(3):
        lat_copy(i).wait_send()
    for k in range(1, SPLIT):
        bg_copy(k).wait_send()

    def sent(k):
        for ph in (FWD, BWD):
            for way in (LEFT, RIGHT):
                for h in range(2):
                    x1_copy(ph, k, way, h, x).wait_send()
                    b_copy(ph, k, way, h == way).wait_send()
                x2_copy(ph, k, way, x).wait_send()
                a_copy(ph, k, way).wait_send()
            c_copy(ph, k).wait_send()

    loop(0, SPLIT, sent)

    def y_sent(k):
        for ph in (FWD, BWD):
            for h in range(2):
                y_copy(ph, k, h).wait_send()

    loop(1, SPLIT, y_sent)


def spread(mix, rows):
    half = rows.shape[-1]
    tile = min(512, half)
    for h in range(2):
        for n in range(0, half, tile):
            block = rows[:, h, :, n:n + tile].reshape(SPLIT * MOST, tile)
            block = jnp.concatenate([block, block], axis=0)
            yield slice(h * half + n, h * half + n + tile), dot_nn(mix[...], block).astype(BF16)


def last_kernel(
    out_v, back_g, mix_g, bg_v, ag_v, out_hbm, grad_hbm, bg_hbm, ag_hbm, grad_v, sem, grad_sem
):
    pairs = ((out_v, out_hbm), (bg_v, bg_hbm), (ag_v, ag_hbm))
    copies = [pltpu.make_async_copy(src, dst, sem.at[i]) for i, (src, dst) in enumerate(pairs)]
    for copy in copies:
        copy.start()
    for i, (cols, value) in enumerate(spread(mix_g, back_g)):
        grad_v[:, cols] = value
        copies.append(pltpu.make_async_copy(grad_v.at[:, cols], grad_hbm.at[:, cols], grad_sem.at[i]))
        copies[-1].start()
    for copy in copies:
        copy.wait()


def on_device(
    section_layer_input, token_expert_choice, route_gate_steps, gate_weight, up_weight, down_weight,
    adapter_down_maps, adapter_up_maps, cotangent,
):
    tokens, width = section_layer_input.shape[1:]
    units = gate_weight.shape[1]
    rank = adapter_down_maps.shape[2]
    half = width // 2
    cols = width // lax.axis_size("expert")
    dma = pltpu.SemaphoreType.DMA
    flight = SPLIT * MOST
    tiles = width // min(512, half)
    hbm = pl.BlockSpec(memory_space=pltpu.HBM)
    vmem = pl.BlockSpec(memory_space=pltpu.VMEM)
    held = pl.pallas_call(
        kernel,
        out_shape=(
            jax.ShapeDtypeStruct((tokens, width), BF16),
            jax.ShapeDtypeStruct((SPLIT, 2, MOST, half), BF16),
            jax.ShapeDtypeStruct((tokens, 2 * flight), BF16),
            jax.ShapeDtypeStruct((SPLIT, rank, cols), F32),
            jax.ShapeDtypeStruct((rank, units), F32),
        ),
        in_specs=[hbm] * 9,
        out_specs=(vmem,) * 5,
        scratch_shapes=[
            pltpu.VMEM((2, tokens, width), BF16),
            pltpu.VMEM((units, width), BF16),
            pltpu.VMEM((units, width), BF16),
            pltpu.VMEM((units, width), BF16),
            pltpu.VMEM((rank, width), BF16),
            pltpu.VMEM((2, SPLIT, 2, MOST, half), BF16),
            pltpu.VMEM((2, SPLIT, 2, SPLIT, MOST, half), BF16),
            pltpu.VMEM((SPLIT, flight, units), F32),
            pltpu.VMEM((SPLIT, flight, units), F32),
            pltpu.VMEM((SPLIT, flight, units), BF16),
            pltpu.VMEM((SPLIT, flight, rank), BF16),
            pltpu.VMEM((2, SPLIT, 2, SPLIT, MOST, half), BF16),
            pltpu.VMEM((2, SPLIT, 2, MOST, half), BF16),
            pltpu.VMEM((2, SPLIT, 2, MOST, half), BF16),
            pltpu.VMEM((2, SPLIT, 2, 2, MOST, half), BF16),
            pltpu.VMEM((2, SPLIT, 2, MOST, half), BF16),
            pltpu.VMEM((SPLIT, 2, MOST, half), BF16),
            pltpu.VMEM((2, tokens, 2 * flight), BF16),
            pltpu.VMEM((tokens, 2 * flight), BF16),
            pltpu.VMEM((rank, SPLIT * flight), BF16),
            pltpu.VMEM((3, rank, SPLIT * flight), BF16),
            pltpu.VMEM((SPLIT, rank, cols), F32),
            pltpu.VMEM(token_expert_choice.shape[:0:-1], jnp.int32),
            pltpu.VMEM(token_expert_choice.shape[:0:-1], jnp.int32),
            pltpu.VMEM((rank, units), BF16),
            dma((9,)),
            dma((2, SPLIT, 2)), dma((2, SPLIT, 2)),
            dma((2, SPLIT, 2, 2)), dma((2, SPLIT, 2, 2)),
            dma((2, SPLIT, 2)), dma((2, SPLIT, 2)),
            dma((2, SPLIT, 2)), dma((2, SPLIT, 2)),
            dma((2, SPLIT, 2, 2)), dma((2, SPLIT, 2, 2)),
            dma((2, SPLIT)), dma((2, SPLIT)),
            dma((2,)), dma((2,)),
            dma((3,)), dma((3,)),
            dma((SPLIT,)), dma((SPLIT,)),
        ],
        compiler_params=pltpu.CompilerParams(
            collective_id=0, has_side_effects=True, vmem_limit_bytes=48 * 1024 * 1024),
    )(
        *[pltpu.with_memory_space_constraint(a, pltpu.HBM) for a in (token_expert_choice[0].T, route_gate_steps[0].T, adapter_down_maps[0].T,
        section_layer_input[0], cotangent[0], gate_weight[0], up_weight[0], down_weight[0],
        adapter_up_maps[0])],
    )
    out, grad, b_grad, a_grad = pl.pallas_call(
        last_kernel,
        out_shape=(
            jax.ShapeDtypeStruct((tokens, width), BF16),
            jax.ShapeDtypeStruct((tokens, width), BF16),
            jax.ShapeDtypeStruct((SPLIT, rank, cols), F32),
            jax.ShapeDtypeStruct((rank, units), F32),
        ),
        in_specs=[vmem] * 5,
        out_specs=(hbm,) * 4,
        scratch_shapes=[pltpu.VMEM((tokens, width), BF16), dma((3,)), dma((tiles,))],
        compiler_params=pltpu.CompilerParams(vmem_limit_bytes=16 * 1024 * 1024),
    )(*held)
    return out[None], grad[None], a_grad.T[None], b_grad[None]


def solution(mesh):
    tokens = P("section", "expert", None)
    return jax.shard_map(
        on_device,
        mesh=mesh,
        in_specs=(tokens,) * 7 + (P("section", None, None, None), tokens),
        out_specs=(tokens, tokens, tokens, P("section", None, None, "expert")),
        check_vma=False,
    )
```

```python
import functools

import jax
import jax.numpy as jnp
from jax import lax
from jax.experimental import pallas as pl
from jax.experimental.pallas import tpu as pltpu
from jax.sharding import PartitionSpec as P

SPLIT = 4
MOST = 16
LOWRANK_SCALE = 2.0
LEVEL_STEP = 1.0 / 4096.0
F32 = jnp.float32
BF16 = jnp.bfloat16
FWD, BWD = 0, 1
LEFT, RIGHT = 0, 1


def dot_nt(a, b):
    return lax.dot_general(a, b, (((1,), (1,)), ((), ())), preferred_element_type=F32)


def dot_nn(a, b):
    return jnp.dot(a, b, preferred_element_type=F32)


def kernel(
    choice_hbm, steps_hbm, at_hbm, tok_hbm, cot_hbm, wg_hbm, wu_hbm, wd_hbm, bup_hbm,
    soon_v, back, mix_in, bg_v, ag_ref,
    rows_v, wg, wu, wd, bup, send, recv, pre_gate_v, pre_up_v, hid_v, lr_v,
    part, from_a, sum_b, from_b, fin, mix, lat, lat_in, bsend, routes, at_v,
    load_sem, sent_sem, y_sem, near_sem, rest_sem, a_sem, b_sem, c_sem, mix_sem, lat_sem, bg_sem,
):
    half = recv.shape[-1]
    units = wg.shape[0]
    tokens = rows_v.shape[1]
    n_section = lax.axis_size("section")
    s = lax.axis_index("section")
    me = lax.axis_index("expert")
    y, x = me // SPLIT, me % SPLIT
    xr, xo, xl = (x + 1) % SPLIT, (x + 2) % SPLIT, (x + 3) % SPLIT
    first, last = 1 - s % 2, s % 2

    def dev(row, col, sec=s):
        return {"section": sec, "expert": row * SPLIT + col}

    def toward(ph):
        return (s + n_section + 1 - 2 * ph) % n_section

    beside = (dev(y, xl), dev(y, xr))

    def copy(src, dst, kind, recv_sem, device):
        return pltpu.make_async_remote_copy(
            src_ref=src, dst_ref=dst, send_sem=sent_sem.at[kind], recv_sem=recv_sem,
            device_id=device, device_id_type=pl.DeviceIdType.MESH,
        )

    def wait(sem, ref):
        pltpu.make_async_copy(ref, ref, sem).wait()

    def loop(first, last, body):
        def step(k, _):
            body(k)
            return 0
        lax.fori_loop(first, last, step, 0)

    loads = [
        pltpu.make_async_copy(src, dst, load_sem.at[i])
        for i, src, dst in (
            (0, choice_hbm, routes.at[0]), (0, steps_hbm, routes.at[1]), (1, tok_hbm, rows_v.at[FWD]),
            (2, cot_hbm, rows_v.at[BWD]), (3, at_hbm, at_v), (4, wg_hbm, wg), (5, wu_hbm, wu),
            (6, wd_hbm, wd), (7, bup_hbm.at[y], bup),
        )
    ]
    for load in loads:
        load.start()

    barrier = pltpu.get_barrier_semaphore()
    partners = [dev(y, xl), dev(y, xr), dev(y, xo)]
    partners += [dev((y + k) % SPLIT, x) for k in range(1, SPLIT)]
    partners += [dev((y + k) % SPLIT, x, sec) for k in range(SPLIT) for sec in (toward(FWD), toward(BWD))]
    for device in partners:
        pl.semaphore_signal(barrier, inc=1, device_id=device, device_id_type=pl.DeviceIdType.MESH)

    shape = (SPLIT * MOST, tokens)
    row = lax.broadcasted_iota(jnp.int32, shape, 0)
    slot = row % MOST
    expert = (y + SPLIT - row // MOST) % SPLIT
    square = (tokens, tokens)
    earlier = lax.broadcasted_iota(jnp.int32, square, 0) < lax.broadcasted_iota(jnp.int32, square, 1)
    earlier = earlier.astype(F32).astype(BF16)
    wait(load_sem.at[0], routes)
    routed = jnp.zeros(shape, jnp.int32)
    gate = jnp.zeros(shape, jnp.int32)
    for j in range(routes.shape[1]):
        hit = routes[0, j:j + 1, :] == expert
        routed = jnp.where(hit, 1, routed)
        gate = jnp.where(hit, routes[1, j:j + 1, :], gate)
    taken = dot_nn(routed.astype(F32).astype(BF16), earlier)
    placed = (routed > 0) & (taken == slot.astype(F32))
    place = jnp.where(placed, 1.0, 0.0).astype(F32)
    weight = place * (gate.astype(F32) * LEVEL_STEP)
    slot_gate = jnp.sum(weight, axis=1, keepdims=True)
    place_half = place.astype(BF16)

    def dispatch(ph):
        for h in range(2):
            out = dot_nn(place_half, rows_v[ph, :, h * half:(h + 1) * half])
            if ph == BWD:
                out = out * slot_gate
            out = out.astype(BF16)
            recv[ph, 0, h, pl.ds(x, 1)] = out[:MOST][None]
            for k in range(1, SPLIT):
                send[ph, k, h] = out[k * MOST:(k + 1) * MOST]

    def y_start(ph, k):
        for h in range(2):
            copy(send.at[ph, k, h], recv.at[ph, k, h, x], ph, y_sem.at[ph, k],
                 dev((y + SPLIT - k) % SPLIT, x)).start()

    def x1_start(ph, k):
        for turn in range(2):
            for way in (LEFT, RIGHT):
                h = way if turn == 0 else 1 - way
                block = recv.at[ph, k, h, x]
                copy(block, block, 2, (near_sem, rest_sem)[turn].at[ph, k], beside[way]).start()

    def y_wait(ph, k):
        wait(y_sem.at[ph, k], send.at[ph, k])
        x1_start(ph, k)

    def x2_start(ph, k):
        wait(near_sem.at[ph, k], from_a.at[ph, k])
        for way in (LEFT, RIGHT):
            block = recv.at[ph, k, way, (xr, xl)[way]]
            copy(block, block, 3, rest_sem.at[ph, k], beside[way]).start()

    def gathered(ph, k):
        wait(rest_sem.at[ph, k], from_b.at[ph, k])

    def a_start(ph, k):
        for way in (LEFT, RIGHT):
            copy(part.at[ph, k, way, xo], from_a.at[ph, k, way], 4, a_sem.at[ph, k],
                 beside[way]).start()

    def b_start(ph, k):
        for way in (LEFT, RIGHT):
            copy(part.at[ph, k, 1 - way, (xl, xr)[way]], from_b.at[ph, k, way, 1 - way], 5,
                 b_sem.at[ph, k], beside[way]).start()

    def relay(ph, k):
        wait(a_sem.at[ph, k], from_a.at[ph, k])
        for way in (LEFT, RIGHT):
            mine = part[ph, k, way, pl.ds((xl, xr)[way], 1)][0].astype(F32)
            sum_b[ph, k, way] = (mine + from_a[ph, k, way].astype(F32)).astype(BF16)
            copy(sum_b.at[ph, k, way], from_b.at[ph, k, way, way], 5, b_sem.at[ph, k],
                 beside[way]).start()

    def finish(ph, k):
        wait(b_sem.at[ph, k], from_b.at[ph, k])
        for h in range(2):
            total = part[ph, k, h, pl.ds(x, 1)][0].astype(F32)
            total = total + from_b[ph, k, LEFT, h].astype(F32) + from_b[ph, k, RIGHT, h].astype(F32)
            fin[ph, k, h] = total.astype(BF16)
        copy(fin.at[ph, k], back.at[ph, k], 6, c_sem.at[ph],
             dev((y + k) % SPLIT, x, toward(ph))).start()

    def rows_of(ph, k, h):
        return recv[ph, k, h].reshape(SPLIT * MOST, half)

    def forward(k):
        pre_gate = dot_nt(rows_of(FWD, k, 0), wg[:, :half]) + dot_nt(rows_of(FWD, k, 1), wg[:, half:])
        pre_up = dot_nt(rows_of(FWD, k, 0), wu[:, :half]) + dot_nt(rows_of(FWD, k, 1), wu[:, half:])
        hidden = (pre_gate * jax.nn.sigmoid(pre_gate) * pre_up).astype(BF16)
        pre_gate_v[k] = pre_gate
        pre_up_v[k] = pre_up
        hid_v[k] = hidden
        latent = dot_nt(hidden, at_v[...]).astype(BF16)
        latent = (LOWRANK_SCALE * latent.astype(F32)).astype(BF16)
        for h in range(2):
            cols = slice(h * half, (h + 1) * half)
            out = dot_nn(hidden, wd[:, cols]) + dot_nn(latent, bup[:, cols])
            part[FWD, k, h] = out.astype(BF16).reshape(SPLIT, MOST, half)

    def backward(k):
        low = dot_nt(rows_of(BWD, k, 0), bup[:, :half]) + dot_nt(rows_of(BWD, k, 1), bup[:, half:])
        low = (LOWRANK_SCALE * low).astype(BF16)
        lr_v[k] = low
        grad_hidden = dot_nt(rows_of(BWD, k, 0), wd[:, :half]) + dot_nt(rows_of(BWD, k, 1), wd[:, half:])
        grad_hidden = grad_hidden + dot_nn(low, at_v[...])
        pre_gate, pre_up = pre_gate_v[k], pre_up_v[k]
        sig = jax.nn.sigmoid(pre_gate)
        grad_gate = (grad_hidden * pre_up * sig * (1.0 + pre_gate * (1.0 - sig))).astype(BF16)
        grad_up = (grad_hidden * pre_gate * sig).astype(BF16)
        for h in range(2):
            cols = slice(h * half, (h + 1) * half)
            out = dot_nn(grad_gate, wg[:, cols]) + dot_nn(grad_up, wu[:, cols])
            part[BWD, k, h] = out.astype(BF16).reshape(SPLIT, MOST, half)

    loads[2].wait()
    dispatch(FWD)
    pl.semaphore_wait(barrier, len(partners))
    x1_start(FWD, 0)
    y_start(FWD, 1)
    y_start(FWD, 3)

    loads[3].wait()
    dispatch(BWD)
    x1_start(BWD, 0)
    y_start(BWD, 1)
    y_start(BWD, 3)
    y_start(FWD, 2)
    y_start(BWD, 2)

    high = weight.astype(BF16).astype(F32)
    mixes = (jnp.concatenate([high, weight - high], axis=0),
             jnp.concatenate([place, jnp.zeros_like(place)], axis=0))
    for ph in (FWD, BWD):
        mix[ph] = jnp.transpose(mixes[ph]).astype(BF16)
        copy(mix.at[ph], mix_in.at[ph], 7, mix_sem.at[ph], dev(y, x, toward(ph))).start()

    def both(step, k):
        step(FWD, k)
        step(BWD, k)

    both(y_wait, 1)
    both(x2_start, 0)
    both(y_wait, 3)
    both(x2_start, 1)
    both(y_wait, 2)
    for load in loads[4:]:
        load.wait()

    def chunk(i):
        return i + i // 2 - 2 * (i // 3)

    def compute_step(i):
        k = chunk(i)
        both(gathered, k)
        forward(k)
        backward(k)
        a_start(first, k)
        b_start(first, k)
        pl.when(i < 2)(lambda: both(x2_start, chunk(i + 2)))
        pl.when(i == 1)(ahead)
        pl.when(i == 2)(lambda: relay(first, 1))

    def ahead():
        relay(first, 0)
        a_start(last, 1)
        b_start(last, 1)

    loop(0, SPLIT, compute_step)
    relay(first, 3)
    a_start(last, 2)
    relay(last, 1)

    hidden_all = hid_v[...].reshape(SPLIT * SPLIT * MOST, units)
    lat[...] = dot_nt(at_v[...], hidden_all).astype(BF16)
    for i, device in enumerate(beside + (dev(y, xo),)):
        copy(lat, lat_in.at[i], 8, lat_sem, device).start()

    relay(first, 2)
    a_start(last, 3)
    b_start(last, 2)
    for k in (0, 1, 3):
        finish(first, k)
    relay(last, 2)
    a_start(last, 0)
    b_start(last, 3)

    ag_ref[...] = lax.dot_general(
        lr_v[...].reshape(SPLIT * SPLIT * MOST, lr_v.shape[-1]),
        hid_v[...].reshape(SPLIT * SPLIT * MOST, units),
        (((0,), (0,)), ((), ())), preferred_element_type=F32)

    width = bg_v.shape[-1]
    wait(lat_sem, lat_in)
    lat_sum = lat[...].astype(F32)
    for i in range(3):
        lat_sum = lat_sum + lat_in[i].astype(F32)
    lat_sum = LOWRANK_SCALE * lat_sum
    lat_high = lat_sum.astype(BF16)
    lat_low = (lat_sum - lat_high.astype(F32)).astype(BF16)

    per_half = half // width
    for k in range(SPLIT):
        block = ((y + k) % SPLIT) * SPLIT + x
        cols = pl.ds(pl.multiple_of((block % per_half) * width, width), width)
        grad_rows = recv[BWD, :, pl.ds(block // per_half, 1), :, :, cols]
        grad_rows = grad_rows.reshape(SPLIT * SPLIT * MOST, width)
        value = dot_nn(lat_high, grad_rows) + dot_nn(lat_low, grad_rows)
        if k == 0:
            bg_v[pl.ds(y, 1)] = value[None]
        else:
            bsend[k] = value
            copy(bsend.at[k], bg_v.at[y], 9, bg_sem, dev((y + k) % SPLIT, x)).start()

    finish(last, 1)
    finish(first, 2)
    relay(last, 3)
    b_start(last, 0)
    finish(last, 2)
    relay(last, 0)
    finish(last, 3)
    finish(last, 0)

    def arrived(ph):
        wait(mix_sem.at[ph], mix_in.at[ph])
        wait(c_sem.at[ph], back.at[ph])

    soon, late = last, first
    arrived(soon)
    for cols, value in spread(mix_in.at[soon], back.at[soon]):
        soon_v[:, cols] = value
    wait(bg_sem, bsend.at[pl.ds(1, SPLIT - 1)])
    for kind, ref in (
        (FWD, send.at[FWD, pl.ds(1, SPLIT - 1)]), (BWD, send.at[BWD, pl.ds(1, SPLIT - 1)]),
        (2, recv.at[FWD]), (3, send), (4, send), (5, recv.at[FWD]), (6, send), (7, mix), (8, lat_in),
        (9, bsend.at[pl.ds(1, SPLIT - 1)]),
    ):
        wait(sent_sem.at[kind], ref)
    arrived(late)


def spread(mix, rows):
    half = rows.shape[-1]
    tile = min(512, half)
    for h in range(2):
        for n in range(0, half, tile):
            block = rows[:, h, :, n:n + tile].reshape(SPLIT * MOST, tile)
            block = jnp.concatenate([block, block], axis=0)
            yield slice(h * half + n, h * half + n + tile), dot_nn(mix[...], block).astype(BF16)


def last_kernel(
    soon_v, back, mix_in, bg_v, ag_v, out_hbm, grad_hbm, bg_hbm, ag_hbm, late_v, sem, late_sem
):
    even = lax.axis_index("section") % 2 == 0
    small = [pltpu.make_async_copy(bg_v, bg_hbm, sem.at[1]), pltpu.make_async_copy(ag_v, ag_hbm, sem.at[2])]

    def write(late, soon_hbm, late_hbm):
        copies = [pltpu.make_async_copy(soon_v, soon_hbm, sem.at[0])]
        copies[0].start()
        for i, (cols, value) in enumerate(spread(mix_in.at[late], back.at[late])):
            late_v[:, cols] = value
            copies.append(
                pltpu.make_async_copy(late_v.at[:, cols], late_hbm.at[:, cols], late_sem.at[i]))
            copies[-1].start()
        for copy in copies:
            copy.wait()

    for copy in small:
        copy.start()
    pl.when(even)(lambda: write(BWD, out_hbm, grad_hbm))
    pl.when(jnp.logical_not(even))(lambda: write(FWD, grad_hbm, out_hbm))
    for copy in small:
        copy.wait()


def on_device(
    section_layer_input, token_expert_choice, route_gate_steps, gate_weight, up_weight, down_weight,
    adapter_down_maps, adapter_up_maps, cotangent,
):
    tokens, width = section_layer_input.shape[1:]
    units = gate_weight.shape[1]
    rank = adapter_down_maps.shape[2]
    half = width // 2
    cols = width // lax.axis_size("expert")
    dma = pltpu.SemaphoreType.DMA
    flight = SPLIT * MOST
    tiles = width // min(512, half)
    hbm = pl.BlockSpec(memory_space=pltpu.HBM)
    vmem = pl.BlockSpec(memory_space=pltpu.VMEM)
    held = pl.pallas_call(
        kernel,
        out_shape=(
            jax.ShapeDtypeStruct((tokens, width), BF16),
            jax.ShapeDtypeStruct((2, SPLIT, 2, MOST, half), BF16),
            jax.ShapeDtypeStruct((2, tokens, 2 * flight), BF16),
            jax.ShapeDtypeStruct((SPLIT, rank, cols), F32),
            jax.ShapeDtypeStruct((rank, units), F32),
        ),
        in_specs=[hbm] * 9,
        out_specs=(vmem,) * 5,
        scratch_shapes=[
            pltpu.VMEM((2, tokens, width), BF16),
            pltpu.VMEM((units, width), BF16),
            pltpu.VMEM((units, width), BF16),
            pltpu.VMEM((units, width), BF16),
            pltpu.VMEM((rank, width), BF16),
            pltpu.VMEM((2, SPLIT, 2, MOST, half), BF16),
            pltpu.VMEM((2, SPLIT, 2, SPLIT, MOST, half), BF16),
            pltpu.VMEM((SPLIT, flight, units), F32),
            pltpu.VMEM((SPLIT, flight, units), F32),
            pltpu.VMEM((SPLIT, flight, units), BF16),
            pltpu.VMEM((SPLIT, flight, rank), BF16),
            pltpu.VMEM((2, SPLIT, 2, SPLIT, MOST, half), BF16),
            pltpu.VMEM((2, SPLIT, 2, MOST, half), BF16),
            pltpu.VMEM((2, SPLIT, 2, MOST, half), BF16),
            pltpu.VMEM((2, SPLIT, 2, 2, MOST, half), BF16),
            pltpu.VMEM((2, SPLIT, 2, MOST, half), BF16),
            pltpu.VMEM((2, tokens, 2 * flight), BF16),
            pltpu.VMEM((rank, SPLIT * flight), BF16),
            pltpu.VMEM((3, rank, SPLIT * flight), BF16),
            pltpu.VMEM((SPLIT, rank, cols), F32),
            pltpu.VMEM((2,) + token_expert_choice.shape[:0:-1], jnp.int32),
            pltpu.VMEM((rank, units), BF16),
            dma((8,)),
            dma((10,)),
            dma((2, SPLIT)),
            dma((2, SPLIT)),
            dma((2, SPLIT)),
            dma((2, SPLIT)),
            dma((2, SPLIT)),
            dma((2,)),
            dma((2,)),
            dma, dma,
        ],
        compiler_params=pltpu.CompilerParams(
            collective_id=0, has_side_effects=True, vmem_limit_bytes=48 * 1024 * 1024),
    )(
        *[pltpu.with_memory_space_constraint(a, pltpu.HBM) for a in (token_expert_choice[0].T, route_gate_steps[0].T, adapter_down_maps[0].T,
        section_layer_input[0], cotangent[0], gate_weight[0], up_weight[0], down_weight[0],
        adapter_up_maps[0])],
    )
    out, grad, b_grad, a_grad = pl.pallas_call(
        last_kernel,
        out_shape=(
            jax.ShapeDtypeStruct((tokens, width), BF16),
            jax.ShapeDtypeStruct((tokens, width), BF16),
            jax.ShapeDtypeStruct((SPLIT, rank, cols), F32),
            jax.ShapeDtypeStruct((rank, units), F32),
        ),
        in_specs=[vmem] * 5,
        out_specs=(hbm,) * 4,
        scratch_shapes=[pltpu.VMEM((tokens, width), BF16), dma((3,)), dma((tiles,))],
        compiler_params=pltpu.CompilerParams(vmem_limit_bytes=16 * 1024 * 1024),
    )(*held)
    return out[None], grad[None], a_grad.T[None], b_grad[None]


def solution(mesh):
    tokens = P("section", "expert", None)
    return jax.shard_map(
        on_device,
        mesh=mesh,
        in_specs=(tokens,) * 7 + (P("section", None, None, None), tokens),
        out_specs=(tokens, tokens, tokens, P("section", None, None, "expert")),
        check_vma=False,
    )
```

```python
import functools

import jax
import jax.numpy as jnp
from jax import lax
from jax.experimental import pallas as pl
from jax.experimental.pallas import tpu as pltpu
from jax.sharding import PartitionSpec as P

SPLIT = 4
MOST = 16
LOWRANK_SCALE = 2.0
LEVEL_STEP = 1.0 / 4096.0
F32 = jnp.float32
BF16 = jnp.bfloat16
FWD, BWD = 0, 1
LEFT, RIGHT = 0, 1


def dot_nt(a, b):
    return lax.dot_general(a, b, (((1,), (1,)), ((), ())), preferred_element_type=F32)


def dot_nn(a, b):
    return jnp.dot(a, b, preferred_element_type=F32)


def kernel(
    choice_hbm, steps_hbm, at_hbm, tok_hbm, cot_hbm, wg_hbm, wu_hbm, wd_hbm, bup_hbm,
    soon_v, back, mix_in, bg_v, ag_ref,
    rows_v, wg, wu, wd, bup, send, recv, pre_gate_v, pre_up_v, hid_v, lr_v,
    part, from_a, sum_b, from_b, fin, mix, lat, lat_in, bsend, routes, at_v,
    load_sem, sent_sem, y_sem, near_sem, rest_sem, a_sem, b_sem, c_sem, mix_sem, lat_sem, bg_sem, ready, go,
):
    half = recv.shape[-1]
    units = wg.shape[0]
    tokens = rows_v.shape[1]
    n_section = lax.axis_size("section")
    s = lax.axis_index("section")
    me = lax.axis_index("expert")
    y, x = me // SPLIT, me % SPLIT
    xr, xo, xl = (x + 1) % SPLIT, (x + 2) % SPLIT, (x + 3) % SPLIT
    first, last = 1 - s % 2, s % 2

    def dev(row, col, sec=s):
        return {"section": sec, "expert": row * SPLIT + col}

    def toward(ph):
        return (s + n_section + 1 - 2 * ph) % n_section

    beside = (dev(y, xl), dev(y, xr))

    def copy(src, dst, kind, recv_sem, device):
        return pltpu.make_async_remote_copy(
            src_ref=src, dst_ref=dst, send_sem=sent_sem.at[kind], recv_sem=recv_sem,
            device_id=device, device_id_type=pl.DeviceIdType.MESH,
        )

    def wait(sem, ref):
        pltpu.make_async_copy(ref, ref, sem).wait()

    def loop(first, last, body):
        def step(k, _):
            body(k)
            return 0
        lax.fori_loop(first, last, step, 0)

    def load(i, src, dst, pieces=1):
        rows = src.shape[0] // pieces
        for piece in range(pieces):
            at = pl.ds(piece * rows, rows)
            pltpu.make_async_copy(src.at[at], dst.at[at], load_sem.at[i]).start()

    load(0, choice_hbm, routes.at[0])
    load(0, steps_hbm, routes.at[1])
    load(1, tok_hbm, rows_v.at[FWD], 4)

    def gate_of(sec):
        return SPLIT * SPLIT - 1 - (SPLIT + 1) * (1 - sec % 2)

    def signal(sem, device):
        pl.semaphore_signal(sem, inc=1, device_id=device, device_id_type=pl.DeviceIdType.MESH)

    n_expert = SPLIT * SPLIT
    gate_me = gate_of(s)
    at_gate = me == gate_me
    elsewhere = jnp.logical_not(at_gate)
    barrier = pltpu.get_barrier_semaphore()

    def tell_all(sem):
        def step(j):
            signal(sem, {"section": s, "expert": (me + j) % n_expert})
        loop(1, n_expert, step)

    def tell_partners():
        partners = [(y, xl), (y, xr), (y, xo)] + [((y + k) % SPLIT, x) for k in range(1, SPLIT)]
        for row, col in partners:
            pl.when(row * SPLIT + col != gate_me)(functools.partial(signal, barrier, dev(row, col)))

    def enter():
        beside_gate = jnp.logical_or(y == gate_me // SPLIT, x == gate_me % SPLIT)
        pl.semaphore_wait(barrier, jnp.where(beside_gate, 2 * SPLIT - 2, 2 * SPLIT - 1))
        signal(ready, {"section": s, "expert": gate_me})

    def enter_gate():
        pl.semaphore_wait(ready, n_expert - 1)
        for ph in (FWD, BWD):
            signal(barrier, {"section": toward(ph), "expert": gate_of(toward(ph))})

    def pass_on():
        pl.semaphore_wait(barrier, 2)
        tell_all(go)

    pl.when(at_gate)(lambda: tell_all(barrier))
    pl.when(elsewhere)(tell_partners)
    load(2, cot_hbm, rows_v.at[BWD], 4)
    weights = ((at_hbm, at_v), (wg_hbm, wg), (wu_hbm, wu), (wd_hbm, wd), (bup_hbm.at[y], bup))
    for i, (src, dst) in enumerate(weights):
        load(3 + i, src, dst)

    shape = (SPLIT * MOST, tokens)
    row = lax.broadcasted_iota(jnp.int32, shape, 0)
    slot = row % MOST
    expert = (y + SPLIT - row // MOST) % SPLIT
    square = (tokens, tokens)
    earlier = lax.broadcasted_iota(jnp.int32, square, 0) < lax.broadcasted_iota(jnp.int32, square, 1)
    earlier = earlier.astype(F32).astype(BF16)
    wait(load_sem.at[0], routes)
    routed = jnp.zeros(shape, jnp.int32)
    gate = jnp.zeros(shape, jnp.int32)
    for j in range(routes.shape[1]):
        hit = routes[0, j:j + 1, :] == expert
        routed = jnp.where(hit, 1, routed)
        gate = jnp.where(hit, routes[1, j:j + 1, :], gate)
    taken = dot_nn(routed.astype(F32).astype(BF16), earlier)
    placed = (routed > 0) & (taken == slot.astype(F32))
    place = jnp.where(placed, 1.0, 0.0).astype(F32)
    weight = place * (gate.astype(F32) * LEVEL_STEP)
    slot_gate = jnp.sum(weight, axis=1, keepdims=True)
    place_half = place.astype(BF16)

    def dispatch(ph):
        for h in range(2):
            out = dot_nn(place_half, rows_v[ph, :, h * half:(h + 1) * half])
            if ph == BWD:
                out = out * slot_gate
            out = out.astype(BF16)
            recv[ph, 0, h, pl.ds(x, 1)] = out[:MOST][None]
            for k in range(1, SPLIT):
                send[ph, k, h] = out[k * MOST:(k + 1) * MOST]

    def y_start(ph, k):
        for h in range(2):
            copy(send.at[ph, k, h], recv.at[ph, k, h, x], ph, y_sem.at[ph, k],
                 dev((y + SPLIT - k) % SPLIT, x)).start()

    def x1_start(ph, k):
        for turn in range(2):
            for way in (LEFT, RIGHT):
                h = way if turn == 0 else 1 - way
                block = recv.at[ph, k, h, x]
                copy(block, block, 2, (near_sem, rest_sem)[turn].at[ph, k], beside[way]).start()

    def y_wait(ph, k):
        wait(y_sem.at[ph, k], send.at[ph, k])
        x1_start(ph, k)

    def x2_start(ph, k):
        wait(near_sem.at[ph, k], from_a.at[ph, k])
        for way in (LEFT, RIGHT):
            block = recv.at[ph, k, way, (xr, xl)[way]]
            copy(block, block, 3, rest_sem.at[ph, k], beside[way]).start()

    def gathered(ph, k):
        wait(rest_sem.at[ph, k], from_b.at[ph, k])

    def a_start(ph, k):
        for way in (LEFT, RIGHT):
            copy(part.at[ph, k, way, xo], from_a.at[ph, k, way], 4, a_sem.at[ph, k],
                 beside[way]).start()

    def b_start(ph, k):
        for way in (LEFT, RIGHT):
            copy(part.at[ph, k, 1 - way, (xl, xr)[way]], from_b.at[ph, k, way, 1 - way], 5,
                 b_sem.at[ph, k], beside[way]).start()

    def relay(ph, k):
        wait(a_sem.at[ph, k], from_a.at[ph, k])
        for way in (LEFT, RIGHT):
            mine = part[ph, k, way, pl.ds((xl, xr)[way], 1)][0].astype(F32)
            sum_b[ph, k, way] = (mine + from_a[ph, k, way].astype(F32)).astype(BF16)
            copy(sum_b.at[ph, k, way], from_b.at[ph, k, way, way], 5, b_sem.at[ph, k],
                 beside[way]).start()

    def finish(ph, k):
        wait(b_sem.at[ph, k], from_b.at[ph, k])
        for h in range(2):
            total = part[ph, k, h, pl.ds(x, 1)][0].astype(F32)
            total = total + from_b[ph, k, LEFT, h].astype(F32) + from_b[ph, k, RIGHT, h].astype(F32)
            fin[ph, k, h] = total.astype(BF16)
        copy(fin.at[ph, k], back.at[ph, k], 6, c_sem.at[ph],
             dev((y + k) % SPLIT, x, toward(ph))).start()

    def rows_of(ph, k, h):
        return recv[ph, k, h].reshape(SPLIT * MOST, half)

    def forward(k):
        pre_gate = dot_nt(rows_of(FWD, k, 0), wg[:, :half]) + dot_nt(rows_of(FWD, k, 1), wg[:, half:])
        pre_up = dot_nt(rows_of(FWD, k, 0), wu[:, :half]) + dot_nt(rows_of(FWD, k, 1), wu[:, half:])
        hidden = (pre_gate * jax.nn.sigmoid(pre_gate) * pre_up).astype(BF16)
        pre_gate_v[k] = pre_gate
        pre_up_v[k] = pre_up
        hid_v[k] = hidden
        latent = dot_nt(hidden, at_v[...]).astype(BF16)
        latent = (LOWRANK_SCALE * latent.astype(F32)).astype(BF16)
        for h in range(2):
            cols = slice(h * half, (h + 1) * half)
            out = dot_nn(hidden, wd[:, cols]) + dot_nn(latent, bup[:, cols])
            part[FWD, k, h] = out.astype(BF16).reshape(SPLIT, MOST, half)

    def backward(k):
        low = dot_nt(rows_of(BWD, k, 0), bup[:, :half]) + dot_nt(rows_of(BWD, k, 1), bup[:, half:])
        low = (LOWRANK_SCALE * low).astype(BF16)
        lr_v[k] = low
        grad_hidden = dot_nt(rows_of(BWD, k, 0), wd[:, :half]) + dot_nt(rows_of(BWD, k, 1), wd[:, half:])
        grad_hidden = grad_hidden + dot_nn(low, at_v[...])
        pre_gate, pre_up = pre_gate_v[k], pre_up_v[k]
        sig = jax.nn.sigmoid(pre_gate)
        grad_gate = (grad_hidden * pre_up * sig * (1.0 + pre_gate * (1.0 - sig))).astype(BF16)
        grad_up = (grad_hidden * pre_gate * sig).astype(BF16)
        for h in range(2):
            cols = slice(h * half, (h + 1) * half)
            out = dot_nn(grad_gate, wg[:, cols]) + dot_nn(grad_up, wu[:, cols])
            part[BWD, k, h] = out.astype(BF16).reshape(SPLIT, MOST, half)

    wait(load_sem.at[1], rows_v.at[FWD])
    dispatch(FWD)
    pl.when(elsewhere)(enter)
    pl.when(at_gate)(enter_gate)
    x1_start(FWD, 0)
    y_start(FWD, 1)
    y_start(FWD, 3)

    wait(load_sem.at[2], rows_v.at[BWD])
    dispatch(BWD)
    x1_start(BWD, 0)
    y_start(BWD, 1)
    y_start(BWD, 3)
    y_start(FWD, 2)
    y_start(BWD, 2)

    high = weight.astype(BF16).astype(F32)
    mixes = (jnp.concatenate([high, weight - high], axis=0),
             jnp.concatenate([place, jnp.zeros_like(place)], axis=0))
    for ph in (FWD, BWD):
        mix[ph] = jnp.transpose(mixes[ph]).astype(BF16)

    def both(step, k):
        step(FWD, k)
        step(BWD, k)

    both(y_wait, 1)
    both(x2_start, 0)
    both(y_wait, 3)
    both(x2_start, 1)
    both(y_wait, 2)
    for i, (_, dst) in enumerate(weights):
        wait(load_sem.at[3 + i], dst)

    def chunk(i):
        return i + i // 2 - 2 * (i // 3)

    def compute_step(i):
        k = chunk(i)
        both(gathered, k)
        forward(k)
        backward(k)
        a_start(first, k)
        b_start(first, k)
        pl.when(i < 2)(lambda: both(x2_start, chunk(i + 2)))
        pl.when(i == 1)(ahead)
        pl.when(i == 2)(lambda: relay(first, 1))

    def ahead():
        relay(first, 0)
        a_start(last, 1)
        b_start(last, 1)

    pl.when(at_gate)(pass_on)
    loop(0, SPLIT, compute_step)
    relay(first, 3)
    a_start(last, 2)
    relay(last, 1)

    hidden_all = hid_v[...].reshape(SPLIT * SPLIT * MOST, units)
    lat[...] = dot_nt(at_v[...], hidden_all).astype(BF16)
    for i, device in enumerate(beside + (dev(y, xo),)):
        copy(lat, lat_in.at[i], 8, lat_sem, device).start()

    relay(first, 2)
    a_start(last, 3)
    b_start(last, 2)
    pl.when(elsewhere)(lambda: pl.semaphore_wait(go, 1))
    for ph in (FWD, BWD):
        copy(mix.at[ph], mix_in.at[ph], 7, mix_sem.at[ph], dev(y, x, toward(ph))).start()
    for k in (0, 1, 3):
        finish(first, k)
    relay(last, 2)
    a_start(last, 0)
    b_start(last, 3)

    ag_ref[...] = lax.dot_general(
        lr_v[...].reshape(SPLIT * SPLIT * MOST, lr_v.shape[-1]),
        hid_v[...].reshape(SPLIT * SPLIT * MOST, units),
        (((0,), (0,)), ((), ())), preferred_element_type=F32)

    width = bg_v.shape[-1]
    wait(lat_sem, lat_in)
    lat_sum = lat[...].astype(F32)
    for i in range(3):
        lat_sum = lat_sum + lat_in[i].astype(F32)
    lat_sum = LOWRANK_SCALE * lat_sum
    lat_high = lat_sum.astype(BF16)
    lat_low = (lat_sum - lat_high.astype(F32)).astype(BF16)

    per_half = half // width
    for k in range(SPLIT):
        block = ((y + k) % SPLIT) * SPLIT + x
        cols = pl.ds(pl.multiple_of((block % per_half) * width, width), width)
        grad_rows = recv[BWD, :, pl.ds(block // per_half, 1), :, :, cols]
        grad_rows = grad_rows.reshape(SPLIT * SPLIT * MOST, width)
        value = dot_nn(lat_high, grad_rows) + dot_nn(lat_low, grad_rows)
        if k == 0:
            bg_v[pl.ds(y, 1)] = value[None]
        else:
            bsend[k] = value
            copy(bsend.at[k], bg_v.at[y], 9, bg_sem, dev((y + k) % SPLIT, x)).start()

    finish(last, 1)
    finish(first, 2)
    relay(last, 3)
    b_start(last, 0)
    finish(last, 2)
    relay(last, 0)
    finish(last, 3)

    def arrived(ph):
        wait(mix_sem.at[ph], mix_in.at[ph])
        wait(c_sem.at[ph], back.at[ph])

    soon, late = last, first
    arrived(soon)
    for cols, value in spread(mix_in.at[soon], back.at[soon]):
        soon_v[:, cols] = value
    finish(last, 0)
    wait(bg_sem, bsend.at[pl.ds(1, SPLIT - 1)])
    for kind, ref in (
        (FWD, send.at[FWD, pl.ds(1, SPLIT - 1)]), (BWD, send.at[BWD, pl.ds(1, SPLIT - 1)]),
        (2, recv.at[FWD]), (3, send), (4, send), (5, recv.at[FWD]), (6, send), (7, mix), (8, lat_in),
        (9, bsend.at[pl.ds(1, SPLIT - 1)]),
    ):
        wait(sent_sem.at[kind], ref)
    arrived(late)


def spread(mix, rows):
    half = rows.shape[-1]
    tile = min(512, half)
    for h in range(2):
        for n in range(0, half, tile):
            block = rows[:, h, :, n:n + tile].reshape(SPLIT * MOST, tile)
            block = jnp.concatenate([block, block], axis=0)
            yield slice(h * half + n, h * half + n + tile), dot_nn(mix[...], block).astype(BF16)


def last_kernel(
    soon_v, back, mix_in, bg_v, ag_v, out_hbm, grad_hbm, bg_hbm, ag_hbm, late_v, sem, late_sem
):
    even = lax.axis_index("section") % 2 == 0
    small = [pltpu.make_async_copy(bg_v, bg_hbm, sem.at[1]), pltpu.make_async_copy(ag_v, ag_hbm, sem.at[2])]

    def write(late, soon_hbm, late_hbm):
        copies = []
        rows = soon_v.shape[0] // 8
        for i in range(8):
            at = pl.ds(i * rows, rows)
            pltpu.make_async_copy(soon_v.at[at], soon_hbm.at[at], sem.at[0]).start()
        for i, (cols, value) in enumerate(spread(mix_in.at[late], back.at[late])):
            late_v[:, cols] = value
            copies.append(
                pltpu.make_async_copy(late_v.at[:, cols], late_hbm.at[:, cols], late_sem.at[i]))
            copies[-1].start()
        for copy in copies:
            copy.wait()
        pltpu.make_async_copy(soon_v, soon_hbm, sem.at[0]).wait()

    for copy in small:
        copy.start()
    pl.when(even)(lambda: write(BWD, out_hbm, grad_hbm))
    pl.when(jnp.logical_not(even))(lambda: write(FWD, grad_hbm, out_hbm))
    for copy in small:
        copy.wait()


def on_device(
    section_layer_input, token_expert_choice, route_gate_steps, gate_weight, up_weight, down_weight,
    adapter_down_maps, adapter_up_maps, cotangent,
):
    tokens, width = section_layer_input.shape[1:]
    units = gate_weight.shape[1]
    rank = adapter_down_maps.shape[2]
    half = width // 2
    cols = width // lax.axis_size("expert")
    dma = pltpu.SemaphoreType.DMA
    flight = SPLIT * MOST
    tiles = width // min(512, half)
    hbm = pl.BlockSpec(memory_space=pltpu.HBM)
    vmem = pl.BlockSpec(memory_space=pltpu.VMEM)
    held = pl.pallas_call(
        kernel,
        out_shape=(
            jax.ShapeDtypeStruct((tokens, width), BF16),
            jax.ShapeDtypeStruct((2, SPLIT, 2, MOST, half), BF16),
            jax.ShapeDtypeStruct((2, tokens, 2 * flight), BF16),
            jax.ShapeDtypeStruct((SPLIT, rank, cols), F32),
            jax.ShapeDtypeStruct((rank, units), F32),
        ),
        in_specs=[hbm] * 9,
        out_specs=(vmem,) * 5,
        scratch_shapes=[
            pltpu.VMEM((2, tokens, width), BF16),
            pltpu.VMEM((units, width), BF16),
            pltpu.VMEM((units, width), BF16),
            pltpu.VMEM((units, width), BF16),
            pltpu.VMEM((rank, width), BF16),
            pltpu.VMEM((2, SPLIT, 2, MOST, half), BF16),
            pltpu.VMEM((2, SPLIT, 2, SPLIT, MOST, half), BF16),
            pltpu.VMEM((SPLIT, flight, units), F32),
            pltpu.VMEM((SPLIT, flight, units), F32),
            pltpu.VMEM((SPLIT, flight, units), BF16),
            pltpu.VMEM((SPLIT, flight, rank), BF16),
            pltpu.VMEM((2, SPLIT, 2, SPLIT, MOST, half), BF16),
            pltpu.VMEM((2, SPLIT, 2, MOST, half), BF16),
            pltpu.VMEM((2, SPLIT, 2, MOST, half), BF16),
            pltpu.VMEM((2, SPLIT, 2, 2, MOST, half), BF16),
            pltpu.VMEM((2, SPLIT, 2, MOST, half), BF16),
            pltpu.VMEM((2, tokens, 2 * flight), BF16),
            pltpu.VMEM((rank, SPLIT * flight), BF16),
            pltpu.VMEM((3, rank, SPLIT * flight), BF16),
            pltpu.VMEM((SPLIT, rank, cols), F32),
            pltpu.VMEM((2,) + token_expert_choice.shape[:0:-1], jnp.int32),
            pltpu.VMEM((rank, units), BF16),
            dma((8,)),
            dma((10,)),
            dma((2, SPLIT)),
            dma((2, SPLIT)),
            dma((2, SPLIT)),
            dma((2, SPLIT)),
            dma((2, SPLIT)),
            dma((2,)),
            dma((2,)),
            dma, dma,
            pltpu.SemaphoreType.REGULAR, pltpu.SemaphoreType.REGULAR,
        ],
        compiler_params=pltpu.CompilerParams(
            collective_id=0, has_side_effects=True, vmem_limit_bytes=48 * 1024 * 1024),
    )(
        *[pltpu.with_memory_space_constraint(a, pltpu.HBM) for a in (token_expert_choice[0].T, route_gate_steps[0].T, adapter_down_maps[0].T,
        section_layer_input[0], cotangent[0], gate_weight[0], up_weight[0], down_weight[0],
        adapter_up_maps[0])],
    )
    out, grad, b_grad, a_grad = pl.pallas_call(
        last_kernel,
        out_shape=(
            jax.ShapeDtypeStruct((tokens, width), BF16),
            jax.ShapeDtypeStruct((tokens, width), BF16),
            jax.ShapeDtypeStruct((SPLIT, rank, cols), F32),
            jax.ShapeDtypeStruct((rank, units), F32),
        ),
        in_specs=[vmem] * 5,
        out_specs=(hbm,) * 4,
        scratch_shapes=[pltpu.VMEM((tokens, width), BF16), dma((3,)), dma((tiles,))],
        compiler_params=pltpu.CompilerParams(vmem_limit_bytes=16 * 1024 * 1024),
    )(*held)
    return out[None], grad[None], a_grad.T[None], b_grad[None]


def solution(mesh):
    tokens = P("section", "expert", None)
    return jax.shard_map(
        on_device,
        mesh=mesh,
        in_specs=(tokens,) * 7 + (P("section", None, None, None), tokens),
        out_specs=(tokens, tokens, tokens, P("section", None, None, "expert")),
        check_vma=False,
    )
```

```python
import functools

import jax
import jax.numpy as jnp
from jax import lax
from jax.experimental import pallas as pl
from jax.experimental.pallas import tpu as pltpu
from jax.sharding import PartitionSpec as P

SPLIT = 4
MOST = 16
LOWRANK_SCALE = 2.0
LEVEL_STEP = 1.0 / 4096.0
F32 = jnp.float32
BF16 = jnp.bfloat16
FWD, BWD = 0, 1
LEFT, RIGHT = 0, 1


def dot_nt(a, b):
    return lax.dot_general(a, b, (((1,), (1,)), ((), ())), preferred_element_type=F32)


def dot_nn(a, b):
    return jnp.dot(a, b, preferred_element_type=F32)


def kernel(
    choice_hbm, steps_hbm, at_hbm, tok_hbm, cot_hbm, wg_hbm, wu_hbm, wd_hbm, bup_hbm,
    soon_v, back, mix_in, bg_v, ag_ref,
    rows_v, wg, wu, wd, bup, send, recv, pre_gate_v, pre_up_v, hid_v, lr_v,
    part, from_a, sum_b, from_b, fin, mix, lat, lat_in, bsend, routes, at_v,
    load_sem, sent_sem, y_sem, near_sem, rest_sem, a_sem, b_sem, c_sem, mix_sem, lat_sem, bg_sem, ready, go,
):
    half = recv.shape[-1]
    units = wg.shape[0]
    tokens = rows_v.shape[1]
    n_section = lax.axis_size("section")
    s = lax.axis_index("section")
    me = lax.axis_index("expert")
    y, x = me // SPLIT, me % SPLIT
    xr, xo, xl = (x + 1) % SPLIT, (x + 2) % SPLIT, (x + 3) % SPLIT
    first, last = 1 - s % 2, s % 2

    def dev(row, col, sec=s):
        return {"section": sec, "expert": row * SPLIT + col}

    def toward(ph):
        return (s + n_section + 1 - 2 * ph) % n_section

    beside = (dev(y, xl), dev(y, xr))

    def copy(src, dst, kind, recv_sem, device):
        return pltpu.make_async_remote_copy(
            src_ref=src, dst_ref=dst, send_sem=sent_sem.at[kind], recv_sem=recv_sem,
            device_id=device, device_id_type=pl.DeviceIdType.MESH,
        )

    def wait(sem, ref):
        pltpu.make_async_copy(ref, ref, sem).wait()

    def loop(first, last, body):
        def step(k, _):
            body(k)
            return 0
        lax.fori_loop(first, last, step, 0)

    def load(i, src, dst, pieces=1):
        rows = src.shape[0] // pieces
        for piece in range(pieces):
            at = pl.ds(piece * rows, rows)
            pltpu.make_async_copy(src.at[at], dst.at[at], load_sem.at[i]).start()

    load(0, choice_hbm, routes.at[0])
    load(0, steps_hbm, routes.at[1])
    load(1, tok_hbm, rows_v.at[FWD], 4)

    def gate_of(sec):
        return SPLIT * SPLIT - 1 - (SPLIT + 1) * (1 - sec % 2)

    def signal(sem, device):
        pl.semaphore_signal(sem, inc=1, device_id=device, device_id_type=pl.DeviceIdType.MESH)

    n_expert = SPLIT * SPLIT
    gate_me = gate_of(s)
    at_gate = me == gate_me
    elsewhere = jnp.logical_not(at_gate)
    barrier = pltpu.get_barrier_semaphore()

    def tell_all(sem):
        def step(j):
            signal(sem, {"section": s, "expert": (me + j) % n_expert})
        loop(1, n_expert, step)

    def tell_partners():
        partners = [(y, xl), (y, xr), (y, xo)] + [((y + k) % SPLIT, x) for k in range(1, SPLIT)]
        for row, col in partners:
            pl.when(row * SPLIT + col != gate_me)(functools.partial(signal, barrier, dev(row, col)))

    def enter():
        beside_gate = jnp.logical_or(y == gate_me // SPLIT, x == gate_me % SPLIT)
        pl.semaphore_wait(barrier, jnp.where(beside_gate, 2 * SPLIT - 2, 2 * SPLIT - 1))
        signal(ready, {"section": s, "expert": gate_me})

    def enter_gate():
        pl.semaphore_wait(ready, n_expert - 1)
        for ph in (FWD, BWD):
            signal(barrier, {"section": toward(ph), "expert": gate_of(toward(ph))})

    def pass_on():
        pl.semaphore_wait(barrier, 2)
        tell_all(go)

    pl.when(at_gate)(lambda: tell_all(barrier))
    pl.when(elsewhere)(tell_partners)
    load(2, cot_hbm, rows_v.at[BWD], 4)
    weights = ((at_hbm, at_v), (wg_hbm, wg), (wu_hbm, wu), (wd_hbm, wd), (bup_hbm.at[y], bup))
    for i, (src, dst) in enumerate(weights):
        load(3 + i, src, dst)

    shape = (SPLIT * MOST, tokens)
    row = lax.broadcasted_iota(jnp.int32, shape, 0)
    slot = row % MOST
    expert = (y + SPLIT - row // MOST) % SPLIT
    square = (tokens, tokens)
    earlier = lax.broadcasted_iota(jnp.int32, square, 0) < lax.broadcasted_iota(jnp.int32, square, 1)
    earlier = earlier.astype(F32).astype(BF16)
    wait(load_sem.at[0], routes)
    routed = jnp.zeros(shape, jnp.int32)
    gate = jnp.zeros(shape, jnp.int32)
    for j in range(routes.shape[1]):
        hit = routes[0, j:j + 1, :] == expert
        routed = jnp.where(hit, 1, routed)
        gate = jnp.where(hit, routes[1, j:j + 1, :], gate)
    taken = dot_nn(routed.astype(F32).astype(BF16), earlier)
    placed = (routed > 0) & (taken == slot.astype(F32))
    place = jnp.where(placed, 1.0, 0.0).astype(F32)
    weight = place * (gate.astype(F32) * LEVEL_STEP)
    slot_gate = jnp.sum(weight, axis=1, keepdims=True)
    place_half = place.astype(BF16)

    def dispatch(ph):
        for h in range(2):
            out = dot_nn(place_half, rows_v[ph, :, h * half:(h + 1) * half])
            if ph == BWD:
                out = out * slot_gate
            out = out.astype(BF16)
            recv[ph, 0, h, pl.ds(x, 1)] = out[:MOST][None]
            for k in range(1, SPLIT):
                send[ph, k, h] = out[k * MOST:(k + 1) * MOST]

    def y_start(ph, k):
        for h in range(2):
            copy(send.at[ph, k, h], recv.at[ph, k, h, x], ph, y_sem.at[ph, k],
                 dev((y + SPLIT - k) % SPLIT, x)).start()

    def x1_start(ph, k):
        for turn in range(2):
            for way in (LEFT, RIGHT):
                h = way if turn == 0 else 1 - way
                block = recv.at[ph, k, h, x]
                copy(block, block, 2, (near_sem.at[ph, k], rest_sem.at[k])[turn], beside[way]).start()

    def y_wait(ph, k):
        wait(y_sem.at[ph, k], send.at[ph, k])
        x1_start(ph, k)

    def x2_start(ph, k):
        wait(near_sem.at[ph, k], from_a.at[ph, k])
        for way in (LEFT, RIGHT):
            block = recv.at[ph, k, way, (xr, xl)[way]]
            copy(block, block, 3, rest_sem.at[k], beside[way]).start()

    def gathered(k):
        wait(rest_sem.at[k], from_b.at[:, k])

    def a_start(ph, k):
        for way in (LEFT, RIGHT):
            copy(part.at[ph, k, way, xo], from_a.at[ph, k, way], 4, a_sem.at[ph, k],
                 beside[way]).start()

    def b_start(ph, k):
        for way in (LEFT, RIGHT):
            copy(part.at[ph, k, 1 - way, (xl, xr)[way]], from_b.at[ph, k, way, 1 - way], 5,
                 b_sem.at[ph, k], beside[way]).start()

    def relay(ph, k):
        wait(a_sem.at[ph, k], from_a.at[ph, k])
        for way in (LEFT, RIGHT):
            mine = part[ph, k, way, pl.ds((xl, xr)[way], 1)][0].astype(F32)
            sum_b[ph, k, way] = (mine + from_a[ph, k, way].astype(F32)).astype(BF16)
            copy(sum_b.at[ph, k, way], from_b.at[ph, k, way, way], 5, b_sem.at[ph, k],
                 beside[way]).start()

    def finish(ph, k):
        wait(b_sem.at[ph, k], from_b.at[ph, k])
        for h in range(2):
            total = part[ph, k, h, pl.ds(x, 1)][0].astype(F32)
            total = total + from_b[ph, k, LEFT, h].astype(F32) + from_b[ph, k, RIGHT, h].astype(F32)
            fin[ph, k, h] = total.astype(BF16)
            copy(fin.at[ph, k, h], back.at[ph, k, h], 6, c_sem.at[ph],
                 dev((y + k) % SPLIT, x, toward(ph))).start()

    def rows_of(ph, k, h):
        return recv[ph, k, h].reshape(SPLIT * MOST, half)

    def forward(k):
        pre_gate = dot_nt(rows_of(FWD, k, 0), wg[:, :half]) + dot_nt(rows_of(FWD, k, 1), wg[:, half:])
        pre_up = dot_nt(rows_of(FWD, k, 0), wu[:, :half]) + dot_nt(rows_of(FWD, k, 1), wu[:, half:])
        hidden = (pre_gate * jax.nn.sigmoid(pre_gate) * pre_up).astype(BF16)
        pre_gate_v[k] = pre_gate
        pre_up_v[k] = pre_up
        hid_v[k] = hidden
        latent = dot_nt(hidden, at_v[...]).astype(BF16)
        latent = (LOWRANK_SCALE * latent.astype(F32)).astype(BF16)
        for h in range(2):
            cols = slice(h * half, (h + 1) * half)
            out = dot_nn(hidden, wd[:, cols]) + dot_nn(latent, bup[:, cols])
            part[FWD, k, h] = out.astype(BF16).reshape(SPLIT, MOST, half)

    def backward(k):
        low = dot_nt(rows_of(BWD, k, 0), bup[:, :half]) + dot_nt(rows_of(BWD, k, 1), bup[:, half:])
        low = (LOWRANK_SCALE * low).astype(BF16)
        lr_v[k] = low
        grad_hidden = dot_nt(rows_of(BWD, k, 0), wd[:, :half]) + dot_nt(rows_of(BWD, k, 1), wd[:, half:])
        grad_hidden = grad_hidden + dot_nn(low, at_v[...])
        pre_gate, pre_up = pre_gate_v[k], pre_up_v[k]
        sig = jax.nn.sigmoid(pre_gate)
        grad_gate = (grad_hidden * pre_up * sig * (1.0 + pre_gate * (1.0 - sig))).astype(BF16)
        grad_up = (grad_hidden * pre_gate * sig).astype(BF16)
        for h in range(2):
            cols = slice(h * half, (h + 1) * half)
            out = dot_nn(grad_gate, wg[:, cols]) + dot_nn(grad_up, wu[:, cols])
            part[BWD, k, h] = out.astype(BF16).reshape(SPLIT, MOST, half)

    wait(load_sem.at[1], rows_v.at[FWD])
    dispatch(FWD)
    pl.when(elsewhere)(enter)
    pl.when(at_gate)(enter_gate)
    x1_start(FWD, 0)
    y_start(FWD, 1)
    y_start(FWD, 3)

    wait(load_sem.at[2], rows_v.at[BWD])
    dispatch(BWD)
    x1_start(BWD, 0)

    high = weight.astype(BF16).astype(F32)
    mixes = (jnp.concatenate([high, weight - high], axis=0),
             jnp.concatenate([place, jnp.zeros_like(place)], axis=0))
    for ph in (FWD, BWD):
        mix[ph] = jnp.transpose(mixes[ph]).astype(BF16)

    def both(step, k):
        step(FWD, k)
        step(BWD, k)

    y_wait(FWD, 1)
    y_start(BWD, 1)
    y_start(BWD, 3)
    x2_start(FWD, 0)
    y_wait(FWD, 3)
    y_start(FWD, 2)
    y_wait(BWD, 1)
    y_start(BWD, 2)
    x2_start(BWD, 0)
    y_wait(BWD, 3)
    both(x2_start, 1)
    both(y_wait, 2)
    for i, (_, dst) in enumerate(weights):
        wait(load_sem.at[3 + i], dst)

    def chunk(i):
        return i + i // 2 - 2 * (i // 3)

    def compute_step(i):
        k = chunk(i)
        gathered(k)
        forward(k)
        backward(k)
        a_start(first, k)
        b_start(first, k)
        pl.when(i < 2)(lambda: both(x2_start, chunk(i + 2)))
        pl.when(i == 1)(ahead)
        pl.when(i == 2)(lambda: relay(first, 1))

    def ahead():
        relay(first, 0)
        a_start(last, 1)
        b_start(last, 1)

    pl.when(at_gate)(pass_on)
    loop(0, SPLIT, compute_step)
    relay(first, 3)
    a_start(last, 2)
    relay(last, 1)

    hidden_all = hid_v[...].reshape(SPLIT * SPLIT * MOST, units)
    lat[...] = dot_nt(at_v[...], hidden_all).astype(BF16)
    for i, device in enumerate(beside + (dev(y, xo),)):
        copy(lat, lat_in.at[i], 8, lat_sem, device).start()

    relay(first, 2)
    a_start(last, 3)
    b_start(last, 2)
    pl.when(elsewhere)(lambda: pl.semaphore_wait(go, 1))
    for ph in (FWD, BWD):
        copy(mix.at[ph], mix_in.at[ph], 7, mix_sem.at[ph], dev(y, x, toward(ph))).start()
    for k in (0, 1, 3):
        finish(first, k)
    relay(last, 2)
    a_start(last, 0)
    b_start(last, 3)

    ag_ref[...] = lax.dot_general(
        lr_v[...].reshape(SPLIT * SPLIT * MOST, lr_v.shape[-1]),
        hid_v[...].reshape(SPLIT * SPLIT * MOST, units),
        (((0,), (0,)), ((), ())), preferred_element_type=F32)

    width = bg_v.shape[-1]
    wait(lat_sem, lat_in)
    lat_sum = lat[...].astype(F32)
    for i in range(3):
        lat_sum = lat_sum + lat_in[i].astype(F32)
    lat_sum = LOWRANK_SCALE * lat_sum
    lat_high = lat_sum.astype(BF16)
    lat_low = (lat_sum - lat_high.astype(F32)).astype(BF16)

    per_half = half // width
    for k in range(SPLIT):
        block = ((y + k) % SPLIT) * SPLIT + x
        cols = pl.ds(pl.multiple_of((block % per_half) * width, width), width)
        grad_rows = recv[BWD, :, pl.ds(block // per_half, 1), :, :, cols]
        grad_rows = grad_rows.reshape(SPLIT * SPLIT * MOST, width)
        value = dot_nn(lat_high, grad_rows) + dot_nn(lat_low, grad_rows)
        if k == 0:
            bg_v[pl.ds(y, 1)] = value[None]
        else:
            bsend[k] = value
            copy(bsend.at[k], bg_v.at[y], 9, bg_sem, dev((y + k) % SPLIT, x)).start()

    finish(last, 1)
    finish(first, 2)
    relay(last, 3)
    b_start(last, 0)
    finish(last, 2)
    relay(last, 0)
    finish(last, 3)

    def arrived(ph):
        wait(mix_sem.at[ph], mix_in.at[ph])
        wait(c_sem.at[ph], back.at[ph])

    soon, late = last, first
    arrived(soon)
    for cols, value in spread(mix_in.at[soon], back.at[soon]):
        soon_v[:, cols] = value
    finish(last, 0)
    wait(bg_sem, bsend.at[pl.ds(1, SPLIT - 1)])
    for kind, ref in (
        (FWD, send.at[FWD, pl.ds(1, SPLIT - 1)]), (BWD, send.at[BWD, pl.ds(1, SPLIT - 1)]),
        (2, recv.at[FWD]), (3, send), (4, send), (5, recv.at[FWD]), (6, send), (7, mix), (8, lat_in),
        (9, bsend.at[pl.ds(1, SPLIT - 1)]),
    ):
        wait(sent_sem.at[kind], ref)
    arrived(late)


def spread(mix, rows):
    half = rows.shape[-1]
    tile = min(512, half)
    for h in range(2):
        for n in range(0, half, tile):
            block = rows[:, h, :, n:n + tile].reshape(SPLIT * MOST, tile)
            block = jnp.concatenate([block, block], axis=0)
            yield slice(h * half + n, h * half + n + tile), dot_nn(mix[...], block).astype(BF16)


def last_kernel(
    soon_v, back, mix_in, bg_v, ag_v, out_hbm, grad_hbm, bg_hbm, ag_hbm, late_v, sem, late_sem
):
    even = lax.axis_index("section") % 2 == 0
    small = [pltpu.make_async_copy(bg_v, bg_hbm, sem.at[1]), pltpu.make_async_copy(ag_v, ag_hbm, sem.at[2])]

    def write(late, soon_hbm, late_hbm):
        copies = []
        rows = soon_v.shape[0] // 8
        for i in range(8):
            at = pl.ds(i * rows, rows)
            pltpu.make_async_copy(soon_v.at[at], soon_hbm.at[at], sem.at[0]).start()
        for i, (cols, value) in enumerate(spread(mix_in.at[late], back.at[late])):
            late_v[:, cols] = value
            copies.append(
                pltpu.make_async_copy(late_v.at[:, cols], late_hbm.at[:, cols], late_sem.at[i]))
            copies[-1].start()
        for copy in copies:
            copy.wait()
        pltpu.make_async_copy(soon_v, soon_hbm, sem.at[0]).wait()

    for copy in small:
        copy.start()
    pl.when(even)(lambda: write(BWD, out_hbm, grad_hbm))
    pl.when(jnp.logical_not(even))(lambda: write(FWD, grad_hbm, out_hbm))
    for copy in small:
        copy.wait()


def on_device(
    section_layer_input, token_expert_choice, route_gate_steps, gate_weight, up_weight, down_weight,
    adapter_down_maps, adapter_up_maps, cotangent,
):
    tokens, width = section_layer_input.shape[1:]
    units = gate_weight.shape[1]
    rank = adapter_down_maps.shape[2]
    half = width // 2
    cols = width // lax.axis_size("expert")
    dma = pltpu.SemaphoreType.DMA
    flight = SPLIT * MOST
    tiles = width // min(512, half)
    hbm = pl.BlockSpec(memory_space=pltpu.HBM)
    vmem = pl.BlockSpec(memory_space=pltpu.VMEM)
    held = pl.pallas_call(
        kernel,
        out_shape=(
            jax.ShapeDtypeStruct((tokens, width), BF16),
            jax.ShapeDtypeStruct((2, SPLIT, 2, MOST, half), BF16),
            jax.ShapeDtypeStruct((2, tokens, 2 * flight), BF16),
            jax.ShapeDtypeStruct((SPLIT, rank, cols), F32),
            jax.ShapeDtypeStruct((rank, units), F32),
        ),
        in_specs=[hbm] * 9,
        out_specs=(vmem,) * 5,
        scratch_shapes=[
            pltpu.VMEM((2, tokens, width), BF16),
            pltpu.VMEM((units, width), BF16),
            pltpu.VMEM((units, width), BF16),
            pltpu.VMEM((units, width), BF16),
            pltpu.VMEM((rank, width), BF16),
            pltpu.VMEM((2, SPLIT, 2, MOST, half), BF16),
            pltpu.VMEM((2, SPLIT, 2, SPLIT, MOST, half), BF16),
            pltpu.VMEM((SPLIT, flight, units), F32),
            pltpu.VMEM((SPLIT, flight, units), F32),
            pltpu.VMEM((SPLIT, flight, units), BF16),
            pltpu.VMEM((SPLIT, flight, rank), BF16),
            pltpu.VMEM((2, SPLIT, 2, SPLIT, MOST, half), BF16),
            pltpu.VMEM((2, SPLIT, 2, MOST, half), BF16),
            pltpu.VMEM((2, SPLIT, 2, MOST, half), BF16),
            pltpu.VMEM((2, SPLIT, 2, 2, MOST, half), BF16),
            pltpu.VMEM((2, SPLIT, 2, MOST, half), BF16),
            pltpu.VMEM((2, tokens, 2 * flight), BF16),
            pltpu.VMEM((rank, SPLIT * flight), BF16),
            pltpu.VMEM((3, rank, SPLIT * flight), BF16),
            pltpu.VMEM((SPLIT, rank, cols), F32),
            pltpu.VMEM((2,) + token_expert_choice.shape[:0:-1], jnp.int32),
            pltpu.VMEM((rank, units), BF16),
            dma((8,)),
            dma((10,)),
            dma((2, SPLIT)),
            dma((2, SPLIT)),
            dma((SPLIT,)),
            dma((2, SPLIT)),
            dma((2, SPLIT)),
            dma((2,)),
            dma((2,)),
            dma, dma,
            pltpu.SemaphoreType.REGULAR, pltpu.SemaphoreType.REGULAR,
        ],
        compiler_params=pltpu.CompilerParams(
            collective_id=0, has_side_effects=True, vmem_limit_bytes=48 * 1024 * 1024),
    )(
        *[pltpu.with_memory_space_constraint(a, pltpu.HBM) for a in (token_expert_choice[0].T, route_gate_steps[0].T, adapter_down_maps[0].T,
        section_layer_input[0], cotangent[0], gate_weight[0], up_weight[0], down_weight[0],
        adapter_up_maps[0])],
    )
    out, grad, b_grad, a_grad = pl.pallas_call(
        last_kernel,
        out_shape=(
            jax.ShapeDtypeStruct((tokens, width), BF16),
            jax.ShapeDtypeStruct((tokens, width), BF16),
            jax.ShapeDtypeStruct((SPLIT, rank, cols), F32),
            jax.ShapeDtypeStruct((rank, units), F32),
        ),
        in_specs=[vmem] * 5,
        out_specs=(hbm,) * 4,
        scratch_shapes=[pltpu.VMEM((tokens, width), BF16), dma((3,)), dma((tiles,))],
        compiler_params=pltpu.CompilerParams(vmem_limit_bytes=16 * 1024 * 1024),
    )(*held)
    return out[None], grad[None], a_grad.T[None], b_grad[None]


def solution(mesh):
    tokens = P("section", "expert", None)
    return jax.shard_map(
        on_device,
        mesh=mesh,
        in_specs=(tokens,) * 7 + (P("section", None, None, None), tokens),
        out_specs=(tokens, tokens, tokens, P("section", None, None, "expert")),
        check_vma=False,
    )
```

```python
import functools

import jax
import jax.numpy as jnp
from jax import lax
from jax.experimental import pallas as pl
from jax.experimental.pallas import tpu as pltpu
from jax.sharding import PartitionSpec as P

SPLIT = 4
MOST = 16
LOWRANK_SCALE = 2.0
LEVEL_STEP = 1.0 / 4096.0
F32 = jnp.float32
BF16 = jnp.bfloat16
FWD, BWD = 0, 1
LEFT, RIGHT = 0, 1


def dot_nt(a, b):
    return lax.dot_general(a, b, (((1,), (1,)), ((), ())), preferred_element_type=F32)


def dot_nn(a, b):
    return jnp.dot(a, b, preferred_element_type=F32)


def kernel(
    choice_hbm, steps_hbm, at_hbm, tok_hbm, cot_hbm, wg_hbm, wu_hbm, wd_hbm, bup_hbm,
    soon_v, back, mix_in, bg_v, ag_ref,
    rows_v, wg, wu, wd, bup, send, recv, pre_gate_v, pre_up_v, hid_v, lr_v,
    part, from_a, sum_b, from_b, fin, mix, lat, lat_in, bsend, routes, at_v,
    load_sem, sent_sem, y_sem, near_sem, rest_sem, a_sem, b_sem, c_sem, mix_sem, lat_sem, bg_sem, ready, go,
):
    half = recv.shape[-1]
    units = wg.shape[0]
    tokens = rows_v.shape[1]
    n_section = lax.axis_size("section")
    s = lax.axis_index("section")
    me = lax.axis_index("expert")
    y, x = me // SPLIT, me % SPLIT
    xr, xo, xl = (x + 1) % SPLIT, (x + 2) % SPLIT, (x + 3) % SPLIT
    first, last = 1 - s % 2, s % 2

    def dev(row, col, sec=s):
        return {"section": sec, "expert": row * SPLIT + col}

    def toward(ph):
        return (s + n_section + 1 - 2 * ph) % n_section

    beside = (dev(y, xl), dev(y, xr))

    def copy(src, dst, kind, recv_sem, device):
        kind = (0, 0, 1, 1, 1, 2, 3, 4, 5, 6)[kind]
        return pltpu.make_async_remote_copy(
            src_ref=src, dst_ref=dst, send_sem=sent_sem.at[kind], recv_sem=recv_sem,
            device_id=device, device_id_type=pl.DeviceIdType.MESH,
        )

    def wait(sem, ref):
        pltpu.make_async_copy(ref, ref, sem).wait()

    def loop(first, last, body):
        def step(k, _):
            body(k)
            return 0
        lax.fori_loop(first, last, step, 0)

    def load(i, src, dst, pieces=1):
        rows = src.shape[0] // pieces
        for piece in range(pieces):
            at = pl.ds(piece * rows, rows)
            pltpu.make_async_copy(src.at[at], dst.at[at], load_sem.at[i]).start()

    load(0, choice_hbm, routes.at[0])
    load(0, steps_hbm, routes.at[1])
    load(1, tok_hbm, rows_v.at[FWD], 4)

    def gate_of(sec):
        return SPLIT * SPLIT - 1 - (SPLIT + 1) * (1 - sec % 2)

    def signal(sem, device):
        pl.semaphore_signal(sem, inc=1, device_id=device, device_id_type=pl.DeviceIdType.MESH)

    n_expert = SPLIT * SPLIT
    gate_me = gate_of(s)
    at_gate = me == gate_me
    elsewhere = jnp.logical_not(at_gate)
    barrier = pltpu.get_barrier_semaphore()

    def tell_all(sem):
        def step(j):
            signal(sem, {"section": s, "expert": (me + j) % n_expert})
        loop(1, n_expert, step)

    def tell_partners():
        partners = [(y, xl), (y, xr), (y, xo)] + [((y + k) % SPLIT, x) for k in range(1, SPLIT)]
        for row, col in partners:
            pl.when(row * SPLIT + col != gate_me)(functools.partial(signal, barrier, dev(row, col)))

    def enter():
        beside_gate = jnp.logical_or(y == gate_me // SPLIT, x == gate_me % SPLIT)
        pl.semaphore_wait(barrier, jnp.where(beside_gate, 2 * SPLIT - 2, 2 * SPLIT - 1))
        signal(ready, {"section": s, "expert": gate_me})

    def enter_gate():
        pl.semaphore_wait(ready, n_expert - 1)
        for ph in (FWD, BWD):
            signal(barrier, {"section": toward(ph), "expert": gate_of(toward(ph))})

    def pass_on():
        pl.semaphore_wait(barrier, 2)
        tell_all(go)

    pl.when(at_gate)(lambda: tell_all(barrier))
    pl.when(elsewhere)(tell_partners)
    load(2, cot_hbm, rows_v.at[BWD], 4)
    weights = ((at_hbm, at_v), (wg_hbm, wg), (wu_hbm, wu), (wd_hbm, wd), (bup_hbm.at[y], bup))
    for i, (src, dst) in enumerate(weights):
        load(3 + i, src, dst)

    shape = (SPLIT * MOST, tokens)
    row = lax.broadcasted_iota(jnp.int32, shape, 0)
    slot = row % MOST
    expert = (y + SPLIT - row // MOST) % SPLIT
    square = (tokens, tokens)
    earlier = lax.broadcasted_iota(jnp.int32, square, 0) < lax.broadcasted_iota(jnp.int32, square, 1)
    earlier = earlier.astype(F32).astype(BF16)
    wait(load_sem.at[0], routes)
    routed = jnp.zeros(shape, jnp.int32)
    gate = jnp.zeros(shape, jnp.int32)
    for j in range(routes.shape[1]):
        hit = routes[0, j:j + 1, :] == expert
        routed = jnp.where(hit, 1, routed)
        gate = jnp.where(hit, routes[1, j:j + 1, :], gate)
    taken = dot_nn(routed.astype(F32).astype(BF16), earlier)
    placed = (routed > 0) & (taken == slot.astype(F32))
    place = jnp.where(placed, 1.0, 0.0).astype(F32)
    weight = place * (gate.astype(F32) * LEVEL_STEP)
    slot_gate = jnp.sum(weight, axis=1, keepdims=True)
    place_half = place.astype(BF16)

    def dispatch(ph):
        for h in range(2):
            out = dot_nn(place_half, rows_v[ph, :, h * half:(h + 1) * half])
            if ph == BWD:
                out = out * slot_gate
            out = out.astype(BF16)
            recv[ph, 0, h, pl.ds(x, 1)] = out[:MOST][None]
            for k in range(1, SPLIT):
                send[ph, k, h] = out[k * MOST:(k + 1) * MOST]

    def y_start(ph, k):
        for h in range(2):
            copy(send.at[ph, k, h], recv.at[ph, k, h, x], ph, y_sem.at[ph, k - 1],
                 dev((y + SPLIT - k) % SPLIT, x)).start()

    def x1_start(ph, k):
        for turn in range(2):
            for way in (LEFT, RIGHT):
                h = way if turn == 0 else 1 - way
                block = recv.at[ph, k, h, x]
                copy(block, block, 2, (near_sem.at[ph, k], rest_sem.at[k])[turn], beside[way]).start()

    def y_wait(ph, k):
        wait(y_sem.at[ph, k - 1], send.at[ph, k])
        x1_start(ph, k)

    def x2_start(ph, k):
        wait(near_sem.at[ph, k], from_a.at[ph, k])
        for way in (LEFT, RIGHT):
            block = recv.at[ph, k, way, (xr, xl)[way]]
            copy(block, block, 3, rest_sem.at[k], beside[way]).start()

    def gathered(k):
        wait(rest_sem.at[k], from_b.at[:, k])

    def a_start(ph, k):
        for way in (LEFT, RIGHT):
            copy(part.at[ph, k, way, xo], from_a.at[ph, k, way], 4, a_sem.at[ph, k],
                 beside[way]).start()

    def b_start(ph, k):
        for way in (LEFT, RIGHT):
            copy(part.at[ph, k, 1 - way, (xl, xr)[way]], from_b.at[ph, k, way, 1 - way], 5,
                 b_sem.at[ph, k], beside[way]).start()

    def relay(ph, k):
        wait(a_sem.at[ph, k], from_a.at[ph, k])
        for way in (LEFT, RIGHT):
            mine = part[ph, k, way, pl.ds((xl, xr)[way], 1)][0].astype(F32)
            sum_b[ph, k, way] = (mine + from_a[ph, k, way].astype(F32)).astype(BF16)
            copy(sum_b.at[ph, k, way], from_b.at[ph, k, way, way], 5, b_sem.at[ph, k],
                 beside[way]).start()

    def finish(ph, k):
        wait(b_sem.at[ph, k], from_b.at[ph, k])
        for h in range(2):
            total = part[ph, k, h, pl.ds(x, 1)][0].astype(F32)
            total = total + from_b[ph, k, LEFT, h].astype(F32) + from_b[ph, k, RIGHT, h].astype(F32)
            fin[ph, k, h] = total.astype(BF16)
            copy(fin.at[ph, k, h], back.at[ph, k, h], 6, c_sem.at[ph],
                 dev((y + k) % SPLIT, x, toward(ph))).start()

    def rows_of(ph, k, h):
        return recv[ph, k, h].reshape(SPLIT * MOST, half)

    def forward(k):
        pre_gate = dot_nt(rows_of(FWD, k, 0), wg[:, :half]) + dot_nt(rows_of(FWD, k, 1), wg[:, half:])
        pre_up = dot_nt(rows_of(FWD, k, 0), wu[:, :half]) + dot_nt(rows_of(FWD, k, 1), wu[:, half:])
        hidden = (pre_gate * jax.nn.sigmoid(pre_gate) * pre_up).astype(BF16)
        pre_gate_v[k] = pre_gate
        pre_up_v[k] = pre_up
        hid_v[k] = hidden
        latent = dot_nt(hidden, at_v[...]).astype(BF16)
        latent = (LOWRANK_SCALE * latent.astype(F32)).astype(BF16)
        for h in range(2):
            cols = slice(h * half, (h + 1) * half)
            out = dot_nn(hidden, wd[:, cols]) + dot_nn(latent, bup[:, cols])
            part[FWD, k, h] = out.astype(BF16).reshape(SPLIT, MOST, half)

    def backward(k):
        low = dot_nt(rows_of(BWD, k, 0), bup[:, :half]) + dot_nt(rows_of(BWD, k, 1), bup[:, half:])
        low = (LOWRANK_SCALE * low).astype(BF16)
        lr_v[k] = low
        grad_hidden = dot_nt(rows_of(BWD, k, 0), wd[:, :half]) + dot_nt(rows_of(BWD, k, 1), wd[:, half:])
        grad_hidden = grad_hidden + dot_nn(low, at_v[...])
        pre_gate, pre_up = pre_gate_v[k], pre_up_v[k]
        sig = jax.nn.sigmoid(pre_gate)
        grad_gate = (grad_hidden * pre_up * sig * (1.0 + pre_gate * (1.0 - sig))).astype(BF16)
        grad_up = (grad_hidden * pre_gate * sig).astype(BF16)
        for h in range(2):
            cols = slice(h * half, (h + 1) * half)
            out = dot_nn(grad_gate, wg[:, cols]) + dot_nn(grad_up, wu[:, cols])
            part[BWD, k, h] = out.astype(BF16).reshape(SPLIT, MOST, half)

    wait(load_sem.at[1], rows_v.at[FWD])
    dispatch(FWD)
    pl.when(elsewhere)(enter)
    pl.when(at_gate)(enter_gate)
    x1_start(FWD, 0)
    y_start(FWD, 1)
    y_start(FWD, 3)

    wait(load_sem.at[2], rows_v.at[BWD])
    dispatch(BWD)
    x1_start(BWD, 0)

    high = weight.astype(BF16).astype(F32)
    mixes = (jnp.concatenate([high, weight - high], axis=0),
             jnp.concatenate([place, jnp.zeros_like(place)], axis=0))
    for ph in (FWD, BWD):
        mix[ph] = jnp.transpose(mixes[ph]).astype(BF16)

    def both(step, k):
        step(FWD, k)
        step(BWD, k)

    y_wait(FWD, 1)
    y_start(BWD, 1)
    y_start(BWD, 3)
    x2_start(FWD, 0)
    y_wait(FWD, 3)
    y_start(FWD, 2)
    y_wait(BWD, 1)
    y_start(BWD, 2)
    x2_start(BWD, 0)
    y_wait(BWD, 3)
    both(x2_start, 1)
    both(y_wait, 2)
    for i, (_, dst) in enumerate(weights):
        wait(load_sem.at[3 + i], dst)

    def chunk(i):
        return i + i // 2 - 2 * (i // 3)

    def compute_step(i):
        k = chunk(i)
        gathered(k)
        forward(k)
        backward(k)
        a_start(first, k)
        b_start(first, k)
        pl.when(i < 2)(lambda: both(x2_start, chunk(i + 2)))
        pl.when(i == 1)(ahead)
        pl.when(i == 2)(lambda: relay(first, 1))

    def ahead():
        relay(first, 0)
        a_start(last, 1)
        b_start(last, 1)

    pl.when(at_gate)(pass_on)
    loop(0, SPLIT, compute_step)
    relay(first, 3)
    a_start(last, 2)
    relay(last, 1)

    hidden_all = hid_v[...].reshape(SPLIT * SPLIT * MOST, units)
    lat[...] = dot_nt(at_v[...], hidden_all).astype(BF16)
    for i, device in enumerate(beside + (dev(y, xo),)):
        copy(lat, lat_in.at[i], 8, lat_sem, device).start()

    relay(first, 2)
    a_start(last, 3)
    b_start(last, 2)
    pl.when(elsewhere)(lambda: pl.semaphore_wait(go, 1))
    for ph in (FWD, BWD):
        copy(mix.at[ph], mix_in.at[ph], 7, mix_sem.at[ph], dev(y, x, toward(ph))).start()
    for k in (0, 1, 3):
        finish(first, k)
    relay(last, 2)
    a_start(last, 0)
    b_start(last, 3)

    ag_ref[...] = lax.dot_general(
        lr_v[...].reshape(SPLIT * SPLIT * MOST, lr_v.shape[-1]),
        hid_v[...].reshape(SPLIT * SPLIT * MOST, units),
        (((0,), (0,)), ((), ())), preferred_element_type=F32)

    width = bg_v.shape[-1]
    wait(lat_sem, lat_in)
    lat_sum = lat[...].astype(F32)
    for i in range(3):
        lat_sum = lat_sum + lat_in[i].astype(F32)
    lat_sum = LOWRANK_SCALE * lat_sum
    lat_high = lat_sum.astype(BF16)
    lat_low = (lat_sum - lat_high.astype(F32)).astype(BF16)

    per_half = half // width
    for k in range(SPLIT):
        block = ((y + k) % SPLIT) * SPLIT + x
        cols = pl.ds(pl.multiple_of((block % per_half) * width, width), width)
        grad_rows = recv[BWD, :, pl.ds(block // per_half, 1), :, :, cols]
        grad_rows = grad_rows.reshape(SPLIT * SPLIT * MOST, width)
        value = dot_nn(lat_high, grad_rows) + dot_nn(lat_low, grad_rows)
        if k == 0:
            bg_v[pl.ds(y, 1)] = value[None]
        else:
            bsend[k] = value
            copy(bsend.at[k], bg_v.at[y], 9, bg_sem, dev((y + k) % SPLIT, x)).start()

    finish(last, 1)
    finish(first, 2)
    relay(last, 3)
    b_start(last, 0)
    finish(last, 2)
    relay(last, 0)
    finish(last, 3)

    def arrived(ph):
        wait(mix_sem.at[ph], mix_in.at[ph])
        wait(c_sem.at[ph], back.at[ph])

    soon, late = last, first
    arrived(soon)
    for cols, value in spread(mix_in.at[soon], back.at[soon]):
        soon_v[:, cols] = value
    finish(last, 0)
    wait(bg_sem, bsend.at[pl.ds(1, SPLIT - 1)])
    for kind, ref in (
        (0, send.at[:, pl.ds(1, SPLIT - 1)]), (1, recv), (2, recv.at[FWD]), (3, send), (4, mix),
        (5, lat_in), (6, bsend.at[pl.ds(1, SPLIT - 1)]),
    ):
        wait(sent_sem.at[kind], ref)
    arrived(late)


def spread(mix, rows):
    half = rows.shape[-1]
    tile = min(512, half)
    for h in range(2):
        for n in range(0, half, tile):
            block = rows[:, h, :, n:n + tile].reshape(SPLIT * MOST, tile)
            block = jnp.concatenate([block, block], axis=0)
            yield slice(h * half + n, h * half + n + tile), dot_nn(mix[...], block).astype(BF16)


def last_kernel(
    soon_v, back, mix_in, bg_v, ag_v, out_hbm, grad_hbm, bg_hbm, ag_hbm, late_v, sem, late_sem
):
    even = lax.axis_index("section") % 2 == 0
    small = [pltpu.make_async_copy(bg_v, bg_hbm, sem.at[1]), pltpu.make_async_copy(ag_v, ag_hbm, sem.at[2])]

    def write(late, soon_hbm, late_hbm):
        copies = []
        rows = soon_v.shape[0] // 8
        for i in range(8):
            at = pl.ds(i * rows, rows)
            pltpu.make_async_copy(soon_v.at[at], soon_hbm.at[at], sem.at[0]).start()
        for i, (cols, value) in enumerate(spread(mix_in.at[late], back.at[late])):
            late_v[:, cols] = value
            copies.append(
                pltpu.make_async_copy(late_v.at[:, cols], late_hbm.at[:, cols], late_sem.at[i]))
            copies[-1].start()
        for copy in copies:
            copy.wait()
        pltpu.make_async_copy(soon_v, soon_hbm, sem.at[0]).wait()

    for copy in small:
        copy.start()
    pl.when(even)(lambda: write(BWD, out_hbm, grad_hbm))
    pl.when(jnp.logical_not(even))(lambda: write(FWD, grad_hbm, out_hbm))
    for copy in small:
        copy.wait()


def on_device(
    section_layer_input, token_expert_choice, route_gate_steps, gate_weight, up_weight, down_weight,
    adapter_down_maps, adapter_up_maps, cotangent,
):
    tokens, width = section_layer_input.shape[1:]
    units = gate_weight.shape[1]
    rank = adapter_down_maps.shape[2]
    half = width // 2
    cols = width // lax.axis_size("expert")
    dma = pltpu.SemaphoreType.DMA
    flight = SPLIT * MOST
    tiles = width // min(512, half)
    hbm = pl.BlockSpec(memory_space=pltpu.HBM)
    vmem = pl.BlockSpec(memory_space=pltpu.VMEM)
    held = pl.pallas_call(
        kernel,
        out_shape=(
            jax.ShapeDtypeStruct((tokens, width), BF16),
            jax.ShapeDtypeStruct((2, SPLIT, 2, MOST, half), BF16),
            jax.ShapeDtypeStruct((2, tokens, 2 * flight), BF16),
            jax.ShapeDtypeStruct((SPLIT, rank, cols), F32),
            jax.ShapeDtypeStruct((rank, units), F32),
        ),
        in_specs=[hbm] * 9,
        out_specs=(vmem,) * 5,
        scratch_shapes=[
            pltpu.VMEM((2, tokens, width), BF16),
            pltpu.VMEM((units, width), BF16),
            pltpu.VMEM((units, width), BF16),
            pltpu.VMEM((units, width), BF16),
            pltpu.VMEM((rank, width), BF16),
            pltpu.VMEM((2, SPLIT, 2, MOST, half), BF16),
            pltpu.VMEM((2, SPLIT, 2, SPLIT, MOST, half), BF16),
            pltpu.VMEM((SPLIT, flight, units), F32),
            pltpu.VMEM((SPLIT, flight, units), F32),
            pltpu.VMEM((SPLIT, flight, units), BF16),
            pltpu.VMEM((SPLIT, flight, rank), BF16),
            pltpu.VMEM((2, SPLIT, 2, SPLIT, MOST, half), BF16),
            pltpu.VMEM((2, SPLIT, 2, MOST, half), BF16),
            pltpu.VMEM((2, SPLIT, 2, MOST, half), BF16),
            pltpu.VMEM((2, SPLIT, 2, 2, MOST, half), BF16),
            pltpu.VMEM((2, SPLIT, 2, MOST, half), BF16),
            pltpu.VMEM((2, tokens, 2 * flight), BF16),
            pltpu.VMEM((rank, SPLIT * flight), BF16),
            pltpu.VMEM((3, rank, SPLIT * flight), BF16),
            pltpu.VMEM((SPLIT, rank, cols), F32),
            pltpu.VMEM((2,) + token_expert_choice.shape[:0:-1], jnp.int32),
            pltpu.VMEM((rank, units), BF16),
            dma((8,)),
            dma((7,)),
            dma((2, SPLIT - 1)),
            dma((2, SPLIT)),
            dma((SPLIT,)),
            dma((2, SPLIT)),
            dma((2, SPLIT)),
            dma((2,)),
            dma((2,)),
            dma, dma,
            pltpu.SemaphoreType.REGULAR, pltpu.SemaphoreType.REGULAR,
        ],
        compiler_params=pltpu.CompilerParams(
            collective_id=0, has_side_effects=True, vmem_limit_bytes=48 * 1024 * 1024),
    )(
        *[pltpu.with_memory_space_constraint(a, pltpu.HBM) for a in (token_expert_choice[0].T, route_gate_steps[0].T, adapter_down_maps[0].T,
        section_layer_input[0], cotangent[0], gate_weight[0], up_weight[0], down_weight[0],
        adapter_up_maps[0])],
    )
    out, grad, b_grad, a_grad = pl.pallas_call(
        last_kernel,
        out_shape=(
            jax.ShapeDtypeStruct((tokens, width), BF16),
            jax.ShapeDtypeStruct((tokens, width), BF16),
            jax.ShapeDtypeStruct((SPLIT, rank, cols), F32),
            jax.ShapeDtypeStruct((rank, units), F32),
        ),
        in_specs=[vmem] * 5,
        out_specs=(hbm,) * 4,
        scratch_shapes=[pltpu.VMEM((tokens, width), BF16), dma((3,)), dma((tiles,))],
        compiler_params=pltpu.CompilerParams(vmem_limit_bytes=16 * 1024 * 1024),
    )(*held)
    return out[None], grad[None], a_grad.T[None], b_grad[None]


def solution(mesh):
    tokens = P("section", "expert", None)
    return jax.shard_map(
        on_device,
        mesh=mesh,
        in_specs=(tokens,) * 7 + (P("section", None, None, None), tokens),
        out_specs=(tokens, tokens, tokens, P("section", None, None, "expert")),
        check_vma=False,
    )
```
